128 devices in a mesh: seq: 16 (over y, x_lo, core), tp: 8 (over z, x_hi).
Axes of the slice: x: 4 (x_hi: 2, x_lo: 2; x = x_hi * 2 + x_lo), y: 4, z: 4, core: 2. Of those that a mesh axis runs over, the one named last changes fastest.
Arguments:
- tokens: bfloat16 [16384, 4096], P('seq', 'tp'), may hold values from -8 to 8
- norm_gain: float32 [4096], replicated, may hold values from 0.1 to 1.9
- w_query: bfloat16 [4096, 4096], P(None, 'tp'), may hold values from -1 to 1
- w_key: bfloat16 [4096, 4096], P(None, 'tp'), may hold values from -1 to 1
- w_value: bfloat16 [4096, 4096], P(None, 'tp'), may hold values from -0.09375 to 0.09375
- w_out: bfloat16 [4096, 4096], P('tp'), may hold values from -0.09375 to 0.09375
- offsets: int32 [5, 32], P(None, 'tp'), may hold values from 0 to 15, as said below
Outputs:
- mixed: bfloat16 [16384, 4096], P('seq', 'tp')
The draws below stay inside these ranges and needn't reach their ends.
Inputs may be any that keep to these rules, and one draw needn't show every extreme that they name: offsets[b, h] lies in 0 to 2**b - 1, and in each branch b every value of that range is taken by some head.
All inputs are finite; a program needn't handle non-finite values.
Results may differ from the reference program's by a relative error of at most 0.0095.
Values may be sent and summed in bfloat16 or wider, within the bound.
No kernel may reach another device: no remote copies, remote signals or barrier semaphores. Data moves between devices by JAX's collectives and lax.ppermute only.
A program may use at most 192 MiB of HBM per device.

```python
import jax
import jax.numpy as jnp
from jax import lax

D = 4096
HEADS = 32
DH = 128
LEVELS = 5
TOKENS = 16384
N_TP = 8


def draw_offsets(key, part):
    level_rows = []
    for level_id in range(LEVELS):
        shuffled = jax.random.permutation(jax.random.fold_in(key, 17 + level_id), HEADS)
        level_rows.append(shuffled % 2 ** level_id)
    return jnp.stack(level_rows).astype(jnp.int32)


def normal_weight(key, salt):
    random_part = jax.random.normal(jax.random.fold_in(key, salt), (D, HEADS * DH), jnp.float32)
    return jnp.clip(random_part, -4.0, 4.0) / D ** 0.5


def draw_w_query(key, part):
    return normal_weight(key, 601).astype(jnp.bfloat16)


def draw_w_key(key, part):
    return normal_weight(key, 602).astype(jnp.bfloat16)


def draw_tokens(key, part):
    return jnp.clip(jax.random.normal(jax.random.fold_in(key, 708), (TOKENS, D), jnp.float32), -6.0, 6.0).astype(jnp.bfloat16)


def block_scale(stream_key, dims, split, least, high):
    def one(position, parts):
        steps = jax.random.uniform(jax.random.fold_in(jax.random.fold_in(stream_key, 6), position), (parts,), jnp.float32, least / len(split), high / len(split))
        return jnp.repeat(jnp.exp(steps), dims[position] // parts).reshape((-1,) + (1,) * (len(dims) - position - 1))

    level = one(*split[0])
    for cut in split[1:]:
        level = level * one(*cut)
    return level


def scatter_about(key, extent, spread, reach, shards=(), dtype=jnp.bfloat16):
    drawn = spread * jax.random.normal(key, extent, jnp.float32)
    if shards:
        drawn = drawn * block_scale(key, extent, shards, -0.22, 0.18)
    return jnp.clip(drawn, -reach, reach).astype(dtype)


def setup_inputs(seed: int = 0) -> dict:
    arg_keys = jax.random.split(jax.random.key(seed), 8)
    tokens = draw_tokens(jax.random.fold_in(arg_keys[7], 71), 0)
    norm_gain = jnp.clip(1.0 + 0.18 * jax.random.normal(arg_keys[1], (D,), jnp.float32), 0.1, 1.9)
    w_query = draw_w_query(jax.random.fold_in(arg_keys[7], 71), 0)
    w_key = draw_w_key(jax.random.fold_in(arg_keys[7], 71), 0)
    w_value = scatter_about(arg_keys[4], (D, HEADS * DH), D ** -0.5, 0.09375, ((1, 8),))
    w_out = scatter_about(arg_keys[5], (HEADS * DH, D), (HEADS * DH) ** -0.5, 0.09375, ((0, 8),))
    offsets = draw_offsets(jax.random.fold_in(arg_keys[7], 71), 0)
    return dict(tokens=tokens, norm_gain=norm_gain, w_query=w_query, w_key=w_key, w_value=w_value, w_out=w_out, offsets=offsets)


def head_output(query_head, key_head, value_head, head_offsets):
    scale = DH ** (-0.5)
    segment = TOKENS // 16
    maxima = []
    totals = []
    sums = []
    for level_id in range(LEVELS):
        dilation = 2 ** level_id
        picked = TOKENS // dilation
        offset = head_offsets[level_id]

        def pick_rows(values):
            shaped = values.reshape(picked, dilation, DH)
            chosen = lax.dynamic_index_in_dim(shaped, offset, 1, keepdims=False)
            return chosen.reshape(picked // segment, segment, DH).astype(jnp.float32)
        query_sel = pick_rows(query_head)
        key_sel = pick_rows(key_head)
        value_sel = pick_rows(value_head)
        scores = jnp.einsum('sqd,skd->sqk', query_sel, key_sel) * scale
        allowed = jnp.tril(jnp.ones((segment, segment), jnp.bool_))
        scores = jnp.where(allowed[None], scores, -jnp.inf)
        row_max = lax.optimization_barrier(jnp.max(scores, -1))
        probs = jnp.exp(scores - row_max[..., None])
        total = lax.optimization_barrier(jnp.sum(probs, -1))
        rounded = lax.optimization_barrier(probs.astype(jnp.bfloat16)).astype(jnp.float32)
        weighted = jnp.einsum('sqk,skd->sqd', rounded, value_sel)
        onehot = jnp.arange(dilation) == offset
        maxima.append(jnp.where(onehot[None, :], row_max.reshape(picked, 1), -jnp.inf).reshape(TOKENS))
        totals.append(jnp.where(onehot[None, :], total.reshape(picked, 1), 0.0).reshape(TOKENS))
        sums.append(jnp.where(onehot[None, :, None], weighted.reshape(picked, 1, DH), 0.0).reshape(TOKENS, DH))
    largest = maxima[0]
    for level_id in range(1, LEVELS):
        largest = jnp.maximum(largest, maxima[level_id])
    denominator = jnp.zeros((TOKENS,), jnp.float32)
    numerator = jnp.zeros((TOKENS, DH), jnp.float32)
    for level_id in range(LEVELS):
        factor = jnp.exp(maxima[level_id] - largest)
        denominator = denominator + factor * totals[level_id]
        numerator = numerator + factor[:, None] * sums[level_id]
    return (numerator / denominator[:, None]).astype(jnp.bfloat16)

def reference(tokens, norm_gain, w_query, w_key, w_value, w_out, offsets):
    tokens_f = tokens.astype(jnp.float32)
    scaled = lax.rsqrt(lax.optimization_barrier(jnp.mean(tokens_f * tokens_f, -1, keepdims=True)) + 1e-05)
    normed = (tokens_f * scaled * norm_gain).astype(jnp.bfloat16)

    def project(weight):
        result = jnp.dot(normed, weight, preferred_element_type=jnp.float32).astype(jnp.bfloat16)
        return result.reshape(TOKENS, HEADS, DH).transpose(1, 0, 2)
    queries = project(w_query)
    key_rows = project(w_key)
    value_rows = project(w_value)

    def one_head(items):
        return head_output(items[0], items[1], items[2], items[3])
    attended = lax.map(one_head, (queries, key_rows, value_rows, offsets.T))
    attended = attended.transpose(1, 0, 2).reshape(TOKENS, HEADS * DH)
    width = HEADS // N_TP * DH
    summed = jnp.zeros((TOKENS, D), jnp.float32)
    for group in range(N_TP):
        partial_term = jnp.dot(attended[:, group * width:(group + 1) * width], w_out[group * width:(group + 1) * width], preferred_element_type=jnp.float32)
        summed = summed + lax.optimization_barrier(partial_term.astype(jnp.bfloat16)).astype(jnp.float32)
    return (tokens_f + summed).astype(jnp.bfloat16)
```

```python
import functools
import math

import jax
import jax.numpy as jnp
from jax import lax
from jax.experimental import pallas as pl
from jax.experimental.pallas import tpu as pltpu
from jax.sharding import PartitionSpec as P

BF16 = jnp.bfloat16
F32 = jnp.float32
LOG2E = math.log2(math.e)
LOW = -1e30
FAR = 1 << 20
VMEM_LIMIT = 56 * 1024 * 1024
SMALL = pl.CostEstimate(flops=1024, bytes_accessed=1024, transcendentals=0)


def z_shift(value, step):
    pairs = [(t, ((t // 2 + step) % 4) * 2 + t % 2) for t in range(8)]
    return lax.ppermute(value, "tp", pairs)


def x_swap(value):
    return lax.ppermute(value, "tp", [(t, t ^ 1) for t in range(8)])


def seq_swap(value, mask):
    return lax.ppermute(value, "seq", [(s, s ^ mask) for s in range(16)])


def gather_x_first(block, *others):
    pair = jnp.stack([block, after(x_swap(block), *others)])
    below = z_shift(pair, 1)
    above = z_shift(pair, -1)
    far_own = z_shift(below[0], 1)
    far_other = z_shift(above[1], -1)
    return [
        (pair, 0, 0, 0),
        (pair, 1, 0, 1),
        (below, 0, -1, 0),
        (below, 1, -1, 1),
        (above, 0, 1, 0),
        (above, 1, 1, 1),
        (far_own, None, 2, 0),
        (far_other, None, 2, 1),
    ]


def gather_z_first(block):
    below = z_shift(block, 1)
    above = z_shift(block, -1)
    other = x_swap(block)
    far = z_shift(below, 1)
    others = x_swap(jnp.stack([below, above, far]))
    return [
        (block, None, 0, 0),
        (below, None, -1, 0),
        (above, None, 1, 0),
        (far, None, 2, 0),
        (other, None, 0, 1),
        (others, 0, -1, 1),
        (others, 1, 1, 1),
        (others, 2, 2, 1),
    ]


def piece_owners(pieces):
    tp = lax.axis_index("tp")
    z, x = tp // 2, tp % 2
    owners = [((z + dz + 4) % 4) * 2 + (x ^ dx) for _, _, dz, dx in pieces]
    return jnp.stack(owners).astype(jnp.int32)


def split_pieces(pieces):
    arrays, where = [], []
    for array, index, _, _ in pieces:
        for number, seen in enumerate(arrays):
            if seen is array:
                break
        else:
            number = len(arrays)
            arrays.append(array)
        where.append((number, index))
    return arrays, where


def whole_spec(array):
    zeros = (0,) * array.ndim
    return pl.BlockSpec(array.shape, lambda *_: zeros)


def copy_pieces(groups, owner_ref, arrays, x_s, sems):
    copies = []
    number = 0
    for row, lane, where, first in groups:
        for array, index in where:
            source = arrays[array] if index is None else arrays[array].at[index]
            rows, depth = source.shape
            low = owner_ref[first + len(copies) - number] * (x_s.shape[1] // 8) + lane
            low = pl.multiple_of(low, depth)
            copies.append(
                pltpu.make_async_copy(
                    source, x_s.at[row : row + rows, pl.ds(low, depth)], sems.at[len(copies)]
                )
            )
            copies[-1].start()
        number = len(copies)
    return copies


def piece_groups(gathers):
    operands, groups, owners = [], [], []
    for row, lane, pieces in gathers:
        arrays, where = split_pieces(pieces)
        where = [(len(operands) + array, index) for array, index in where]
        groups.append((row, lane, where, 8 * len(owners)))
        operands += arrays
        owners.append(piece_owners(pieces))
    return operands, groups, jnp.concatenate(owners)


def pick_places(levels, tokens, first, rows):
    unit = tokens // 16
    places = []
    base = 0
    for level in range(1, levels):
        count = rows >> level
        at = base + (first >> level)
        lows = [
            at,
            at - 8 * unit if level == 2 else None,
            at - 12 * unit if level >= 3 else None,
            at - 14 * unit if level == 4 else None,
        ]
        places.append((count, lows))
        base += tokens >> level
    return places


def keys_kernel(groups, n_arrays, n_old, first, heads, levels, *refs):
    owner_ref, offset_ref = refs[:2]
    arrays = refs[2 : 2 + n_arrays]
    gain_ref, wk_ref, wv_ref = refs[2 + n_arrays : 5 + n_arrays]
    refs = refs[5 + n_arrays + n_old :]
    x_out, k_out, v_out = refs[:3]
    picks = refs[3:7]
    x_s, w_s, kv_s, split_s, pick_s, piece_sems, w_sems, x_sem, kv_sems, pick_sems = refs[7:]
    rows, depth = x_s.shape
    tokens = k_out.shape[0]

    copies = copy_pieces(groups, owner_ref, arrays, x_s, piece_sems)
    w_copies = []
    for i, w_ref in enumerate((wk_ref, wv_ref)):
        for k in range(4):
            part = slice(k * depth // 4, (k + 1) * depth // 4)
            w_copies.append(pltpu.make_async_copy(w_ref.at[part], w_s.at[i, part], w_sems.at[i, k]))
            w_copies[-1].start()
    for copy in copies:
        copy.wait()

    def normalise(i, carry):
        at = pl.ds(pl.multiple_of(i * 32, 32), 32)
        value = x_s[at, :].astype(F32)
        scaled = lax.rsqrt(jnp.mean(value * value, -1, keepdims=True) + 1e-05)
        x_s[at, :] = (value * scaled * gain_ref[...]).astype(BF16)
        return carry

    lax.fori_loop(0, rows // 32, normalise, 0, unroll=2)
    here = slice(first, first + rows)
    waits = [pltpu.make_async_copy(x_s, x_out.at[here], x_sem)]
    waits[0].start()

    for i, out in enumerate((k_out, v_out)):
        for copy in w_copies[4 * i : 4 * i + 4]:
            copy.wait()
        full = jnp.dot(x_s[...], w_s[i], preferred_element_type=F32)
        kv_s[i] = full.astype(BF16)
        waits.append(pltpu.make_async_copy(kv_s.at[i], out.at[here], kv_sems.at[i]))
        waits[-1].start()
        for head in range(heads):
            split_s[i * heads + head] = full[:, head * 128 : head * 128 + 128]

    local = 0
    for level, (count, lows) in enumerate(pick_places(levels, tokens, first, rows), 1):
        for head in range(heads):
            start = offset_ref[level, head]
            for side in range(2):
                lane = (side * heads + head) * 128
                pick_s[local : local + count, lane : lane + 128] = split_s[
                    side * heads + head, pl.ds(start, count, stride=2**level), :
                ].astype(BF16)
        for which, low in enumerate(lows):
            if low is not None:
                waits.append(
                    pltpu.make_async_copy(
                        pick_s.at[local : local + count],
                        picks[which].at[low : low + count],
                        pick_sems.at[level - 1, which],
                    )
                )
                waits[-1].start()
        local += count
    for copy in waits:
        copy.wait()


def keys(gathers, first, rows, tokens, old, norm_gain, w_key, w_value, offsets):
    operands, groups, owners = piece_groups(gathers)
    depth, width = w_key.shape
    levels, heads = offsets.shape
    unit = tokens // 16
    outs = [jax.ShapeDtypeStruct((tokens, depth), BF16)]
    outs += [jax.ShapeDtypeStruct((tokens, width), BF16)] * 2
    outs += [jax.ShapeDtypeStruct((n * unit, 2 * width), BF16) for n in (15, 4, 3, 1)]
    anywhere = pl.BlockSpec(memory_space=pl.ANY)
    scalars = pl.BlockSpec(memory_space=pltpu.SMEM)
    vector = pl.BlockSpec(memory_space=pltpu.VMEM)
    before = 5 + len(operands)
    return pl.pallas_call(
        functools.partial(keys_kernel, groups, len(operands), len(old), first, heads, levels),
        in_specs=[scalars, scalars]
        + [anywhere] * len(operands)
        + [vector]
        + [anywhere] * (2 + len(old)),
        out_specs=[anywhere for _ in outs],
        scratch_shapes=[
            pltpu.VMEM((rows, depth), BF16),
            pltpu.VMEM((2, depth, width), BF16),
            pltpu.VMEM((2, rows, width), BF16),
            pltpu.VMEM((2 * heads, rows, 128), F32),
            pltpu.VMEM((rows * 15 // 16, 2 * width), BF16),
            pltpu.SemaphoreType.DMA((8 * len(groups),)),
            pltpu.SemaphoreType.DMA((2, 4)),
            pltpu.SemaphoreType.DMA,
            pltpu.SemaphoreType.DMA((2,)),
            pltpu.SemaphoreType.DMA((levels - 1, 4)),
        ],
        out_shape=outs,
        input_output_aliases={before + i: i for i in range(len(old))},
        compiler_params=pltpu.CompilerParams(vmem_limit_bytes=VMEM_LIMIT),
        cost_estimate=SMALL,
        name="keys",
    )(owners, offsets, *operands, norm_gain[None], w_key, w_value, *old)


def queries_kernel(q_scale, x_ref, w_ref, out_ref):
    full = jnp.dot(x_ref[...], w_ref[...], preferred_element_type=F32)
    out_ref[...] = (full * q_scale).astype(BF16)


def queries(normed, w_query, heads):
    tokens, depth = normed.shape
    width = w_query.shape[1]
    tile = 256
    return pl.pallas_call(
        functools.partial(queries_kernel, LOG2E * (width // heads) ** (-0.5)),
        grid=(tokens // tile,),
        in_specs=[
            pl.BlockSpec((tile, depth), lambda i: (i, 0)),
            pl.BlockSpec((depth, width), lambda i: (0, 0)),
        ],
        out_specs=pl.BlockSpec((tile, width), lambda i: (i, 0)),
        out_shape=jax.ShapeDtypeStruct((tokens, width), BF16),
        compiler_params=pltpu.CompilerParams(vmem_limit_bytes=VMEM_LIMIT),
        cost_estimate=SMALL,
        name="queries",
    )(normed, w_query)


def exchange(own, second, p34, fourth, ready_1, ready_2):
    unit = fourth.shape[0]
    by_x = seq_swap(p34, 2)
    by_y = seq_swap(p34, 4)
    by_x2 = seq_swap(second, 2)
    by_y2 = seq_swap(fourth, 8)
    by_y3 = seq_swap(fourth, 12)
    core_own = seq_swap(own, 1)
    by_x = after(by_x, ready_1)
    by_yx = seq_swap(by_x, 4)
    x_fourth = by_x[2 * unit :]
    by_y2x = seq_swap(x_fourth, 8)
    by_y3x = seq_swap(x_fourth, 12)
    others = jnp.concatenate(
        [by_x, by_y, by_yx, by_x2, by_y2, by_y3, by_y2x, by_y3x]
    )
    others = after(others, ready_2)
    core_others = seq_swap(others, 1)
    return own, core_own, others, core_others


def level_blocks(level, unit):
    count = unit * (16 >> level)
    base = unit * (0, 0, 8, 12, 14)[level]
    blocks = [(0, base, count, 0), (1, base, count, 1)]
    other = []
    if level == 2:
        other.append((9, 2))
    if level >= 3:
        other += [((0, 2)[level - 3] + 3 * i, m) for i, m in enumerate((2, 4, 6))]
    if level == 4:
        other += [(13 + i, m) for i, m in enumerate((8, 12, 10, 14))]
    for low, mask in other:
        blocks += [(2, low * unit, count, mask), (3, low * unit, count, mask + 1)]
    return blocks


def key_table(unit, levels):
    position = lax.axis_index("seq")
    rows = []
    for level in range(1, levels):
        columns = []
        for _, _, count, mask in level_blocks(level, unit):
            if mask == 0:
                columns.append(jnp.arange(count, dtype=jnp.int32))
            else:
                top = 1 << (mask.bit_length() - 1)
                columns.append(jnp.full((count,), jnp.where((position & top) != 0, -1, FAR), jnp.int32))
        rows.append(jnp.concatenate(columns))
    return jnp.stack(rows)


TILE = 256
NT = (((1,), (1,)), ((), ()))


def local_kernel(q_ref, k_ref, v_ref, m_ref, l_ref, a_ref, v_s):
    tokens = q_ref.shape[0]
    v_s[:, :128] = v_ref[...]
    v_s[:, 128:] = jnp.ones((tokens, 128), BF16)
    lower = lax.broadcasted_iota(jnp.int32, (TILE, TILE), 0) >= lax.broadcasted_iota(
        jnp.int32, (TILE, TILE), 1
    )
    for number in range(tokens // TILE):
        low, high = number * TILE, number * TILE + TILE
        query = q_ref[low:high, :]
        own = lax.dot_general(query, k_ref[low:high, :], NT, preferred_element_type=F32)
        scores = jnp.where(lower, own, LOW)
        if number:
            before = lax.dot_general(query, k_ref[:low, :], NT, preferred_element_type=F32)
            scores = jnp.concatenate([before, scores], 1)
        top = jnp.max(scores, 1, keepdims=True)
        probs = jnp.exp2(scores - top).astype(BF16)
        both = jnp.dot(probs, v_s[:high, :], preferred_element_type=F32)
        m_ref[low:high, :] = jnp.broadcast_to(top, (TILE, 128))
        a_ref[low:high, :] = both[:, :128]
        l_ref[low:high, :] = both[:, 128:]


def attend_local(q, k, v):
    tokens, width = q.shape
    block = pl.BlockSpec((tokens, 128), lambda h: (0, h))
    return pl.pallas_call(
        local_kernel,
        grid=(width // 128,),
        in_specs=[block] * 3,
        out_specs=[block] * 3,
        scratch_shapes=[pltpu.VMEM((tokens, 256), BF16)],
        out_shape=[jax.ShapeDtypeStruct((tokens, width), F32)] * 3,
        compiler_params=pltpu.CompilerParams(vmem_limit_bytes=VMEM_LIMIT),
        cost_estimate=SMALL,
        name="attend_local",
    )(q, k, v)


def attend_kernel(levels, head_base, *refs):
    offset_ref, q_ref, m_ref, l_ref, a_ref = refs[:5]
    k_group, v_group = refs[5:9], refs[9:13]
    table_ref, out_ref, q_f, k_s, v_s, m_s, l_s, a_s = refs[13:]
    head = head_base + pl.program_id(0)
    tokens = q_f.shape[0]
    unit = k_group[0].shape[0] // 15
    q_f[...] = q_ref[...].astype(F32)
    m_s[...] = m_ref[...]
    l_s[...] = l_ref[...]
    a_s[...] = a_ref[...]
    v_s[:, 128:] = jnp.ones((tokens, 128), BF16)

    for level in range(1, levels):
        dilation = 2**level
        picked = tokens // dilation
        start = offset_ref[level, head]
        row = 0
        for source, low, count, _ in level_blocks(level, unit):
            k_s[row : row + count, :] = k_group[source][low : low + count, :]
            v_s[row : row + count, :128] = v_group[source][low : low + count, :]
            row += count
        order = table_ref[level - 1 : level, :]
        size = min(TILE, picked)
        for number in range(picked // size):
            rows = pl.ds(start + number * size * dilation, size, stride=dilation)
            query = q_f[rows, :].astype(BF16)
            scores = lax.dot_general(query, k_s[...], NT, preferred_element_type=F32)
            at = lax.broadcasted_iota(jnp.int32, (size, tokens), 0) + number * size
            scores = jnp.where(order <= at, scores, LOW)
            m_old = m_s[rows, :]
            top = jnp.maximum(m_old[:, :1], jnp.max(scores, 1, keepdims=True))
            probs = jnp.exp2(scores - top).astype(BF16)
            both = jnp.dot(probs, v_s[...], preferred_element_type=F32)
            factor = jnp.exp2(m_old - top)
            m_s[rows, :] = jnp.broadcast_to(top, (size, 128))
            a_s[rows, :] = factor * a_s[rows, :] + both[:, :128]
            l_s[rows, :] = factor * l_s[rows, :] + both[:, 128:]

    out_ref[...] = (a_s[...] / l_s[...]).astype(BF16)


def attend(q, state, exchanged, table, offsets, head_base):
    levels, heads = offsets.shape
    tokens = q.shape[0]
    half = heads // 2
    mine = pl.BlockSpec((tokens, 128), lambda h, offset: (0, h + head_base))

    def group_spec(array, shift):
        return pl.BlockSpec((array.shape[0], 128), lambda h, offset: (0, h + shift))

    return pl.pallas_call(
        functools.partial(attend_kernel, levels, head_base),
        grid_spec=pltpu.PrefetchScalarGridSpec(
            num_scalar_prefetch=1,
            grid=(half,),
            in_specs=[mine] * 4
            + [group_spec(a, head_base) for a in exchanged]
            + [group_spec(a, heads + head_base) for a in exchanged]
            + [whole_spec(table)],
            out_specs=pl.BlockSpec((tokens, 128), lambda h, offset: (0, h)),
            scratch_shapes=[
                pltpu.VMEM((tokens, 128), F32),
                pltpu.VMEM((tokens, 128), BF16),
                pltpu.VMEM((tokens, 256), BF16),
                pltpu.VMEM((tokens, 128), F32),
                pltpu.VMEM((tokens, 128), F32),
                pltpu.VMEM((tokens, 128), F32),
            ],
        ),
        out_shape=jax.ShapeDtypeStruct((tokens, 128 * half), BF16),
        compiler_params=pltpu.CompilerParams(vmem_limit_bytes=VMEM_LIMIT),
        cost_estimate=SMALL,
        name="attend",
    )(offsets, q, *state, *exchanged, *exchanged, table)


def output_kernel(group, n_arrays, share, *refs):
    owner_ref, refs = refs[0], refs[1:]
    arrays, refs = refs[:n_arrays], refs[n_arrays:]
    base_ref, w_ref, out_ref, x_s, w_s, piece_sems, w_sems = refs
    copies = copy_pieces([group], owner_ref, arrays, x_s, piece_sems)
    for i in range(w_s.shape[1]):
        copies.append(pltpu.make_async_copy(w_ref.at[share + i], w_s.at[:, i], w_sems.at[i]))
        copies[-1].start()
    for copy in copies:
        copy.wait()
    tile = 512
    rows, depth = x_s.shape

    @pl.loop(0, rows // tile)
    def _(n):
        at = pl.ds(pl.multiple_of(n * tile, tile), tile)
        weight = w_s[...].reshape(depth, out_ref.shape[1])
        total = jnp.dot(x_s[at, :], weight, preferred_element_type=F32)
        out_ref[at, :] = (base_ref[at, :].astype(F32) + total).astype(out_ref.dtype)


def output(pieces, base, w_columns, share, dtype):
    operands, groups, owners = piece_groups([(0, 0, pieces)])
    rows, width = base.shape
    shares = w_columns.shape[0] // 2
    depth = w_columns.size // width // 2
    anywhere = pl.BlockSpec(memory_space=pl.ANY)
    vector = pl.BlockSpec(memory_space=pltpu.VMEM)
    return pl.pallas_call(
        functools.partial(output_kernel, groups[0], len(operands), share),
        in_specs=[pl.BlockSpec(memory_space=pltpu.SMEM)]
        + [anywhere] * len(operands)
        + [vector, anywhere],
        out_specs=vector,
        scratch_shapes=[
            pltpu.VMEM((rows, depth), BF16),
            pltpu.VMEM((w_columns.shape[1], shares) + w_columns.shape[2:], BF16),
            pltpu.SemaphoreType.DMA((8,)),
            pltpu.SemaphoreType.DMA((shares,)),
        ],
        out_shape=jax.ShapeDtypeStruct((rows, width), dtype),
        compiler_params=pltpu.CompilerParams(vmem_limit_bytes=VMEM_LIMIT),
        cost_estimate=SMALL,
        name="output",
    )(owners, *operands, base, w_columns)


def column_shares(w_out):
    seq = lax.axis_index("seq")
    share = seq // 4 * 2 + seq % 2
    rows = w_out.shape[0] // 8
    part = lax.dynamic_slice_in_dim(w_out, share * rows, rows, 0)
    width = w_out.shape[1] // 8
    cut = part.reshape(rows, 8, width).transpose(1, 0, 2)
    return lax.all_to_all(cut, "tp", 0, 0, tiled=True)


def gather_shares(mine):
    groups = [[y * 4 + x_lo * 2 + core for y in range(4) for core in range(2)] for x_lo in range(2)]
    return lax.all_gather(mine, "seq", axis=0, axis_index_groups=groups)


def after(value, *others):
    return lax.optimization_barrier((value, *others))[0]


def on_device(tokens, norm_gain, w_query, w_key, w_value, w_out, offsets):
    rows = tokens.shape[0]
    levels, heads = offsets.shape
    quarter = rows // 4
    spans = ((0, quarter), (quarter, 2 * quarter), (3 * quarter, quarter))

    def keys_of(number, pieces, old):
        low, count = spans[number]
        return keys([(0, 0, pieces)], low, count, rows, old, norm_gain, w_key, w_value, offsets)

    first = gather_z_first(tokens[:quarter])
    second = gather_x_first(tokens[quarter : 3 * quarter], first[1][0], first[2][0])
    mine = column_shares(after(w_out, first[3][0]))
    old = keys_of(0, first, [])
    third = gather_x_first(tokens[3 * quarter :], old[0])
    w_columns = gather_shares(after(mine, old[1]))
    old = keys_of(1, second, old)
    old = keys_of(2, third, old)
    normed, k, v = old[:3]
    q = queries(normed, w_query, heads)
    state = attend_local(q, k, v)
    exchanged = exchange(*old[3:], q, state[0])
    table = key_table(rows // 16, levels)
    gathered = []
    for number, gather in enumerate((gather_z_first, gather_x_first)):
        attended = attend(q, state, exchanged, table, offsets, number * heads // 2)
        gathered.append(gather(attended))
    total = output(gathered[1], tokens, w_columns, 4, F32)
    return output(gathered[0], total, w_columns, 0, BF16)


def solution(mesh):
    placed = (
        P("seq", "tp"),
        P(),
        P(None, "tp"),
        P(None, "tp"),
        P(None, "tp"),
        P("tp", None),
        P(None, "tp"),
    )
    return jax.shard_map(
        on_device, mesh=mesh, in_specs=placed, out_specs=P("seq", "tp"), check_vma=False
    )
```

```python
import functools
import math

import jax
import jax.numpy as jnp
from jax import lax
from jax.experimental import pallas as pl
from jax.experimental.pallas import tpu as pltpu
from jax.sharding import PartitionSpec as P

BF16 = jnp.bfloat16
F32 = jnp.float32
LOG2E = math.log2(math.e)
LOW = -1e30
FAR = 1 << 20
VMEM_LIMIT = 56 * 1024 * 1024
FLOPS_PER_US = 1000000000
F1 = 0
F3 = 1
F4 = 1
F7 = 1
F8 = 0
F9 = 0
CO = 30
CA = 9
C0 = 12
C1 = 20
C2 = 8
F5 = 1
F6 = 0


def cost(us):
    return pl.CostEstimate(flops=int(us * FLOPS_PER_US), bytes_accessed=1024, transcendentals=0)


def z_shift(value, step):
    pairs = [(t, ((t // 2 + step) % 4) * 2 + t % 2) for t in range(8)]
    return lax.ppermute(value, "tp", pairs)


def x_swap(value):
    return lax.ppermute(value, "tp", [(t, t ^ 1) for t in range(8)])


def seq_swap(value, mask):
    return lax.ppermute(value, "seq", [(s, s ^ mask) for s in range(16)])


def x_first_pieces(pair, below, above, far_own, far_other):
    return [
        (pair, 0, 0, 0),
        (pair, 1, 0, 1),
        (below, 0, -1, 0),
        (below, 1, -1, 1),
        (above, 0, 1, 0),
        (above, 1, 1, 1),
        (far_own, None, 2, 0),
        (far_other, None, 2, 1),
    ]


def z_first_pieces(block, below, above, far, other, others, other_far=None):
    return [
        (block, None, 0, 0),
        (below, None, -1, 0),
        (above, None, 1, 0),
        (far, None, 2, 0),
        (other, None, 0, 1),
        (others, 0, -1, 1),
        (others, 1, 1, 1),
        (others, 2, 2, 1) if other_far is None else (other_far, None, 2, 1),
    ]


def piece_owners(pieces):
    tp = lax.axis_index("tp")
    z, x = tp // 2, tp % 2
    owners = [((z + dz + 4) % 4) * 2 + (x ^ dx) for _, _, dz, dx in pieces]
    return jnp.stack(owners).astype(jnp.int32)


def split_pieces(pieces):
    arrays, where = [], []
    for array, index, _, _ in pieces:
        for number, seen in enumerate(arrays):
            if seen is array:
                break
        else:
            number = len(arrays)
            arrays.append(array)
        where.append((number, index))
    return arrays, where


def whole_spec(array):
    zeros = (0,) * array.ndim
    return pl.BlockSpec(array.shape, lambda *_: zeros)


def copy_pieces(where, owner_ref, arrays, x_s, sems, owned):
    copies = []
    for number, (array, index) in enumerate(where):
        source = arrays[array] if index is None else arrays[array].at[index]
        depth = source.shape[1]
        place = owner_ref[number] if owned else number
        low = pl.multiple_of(place * depth, depth) if owned else number * depth
        copies.append(
            pltpu.make_async_copy(source, x_s.at[:, pl.ds(low, depth)], sems.at[number])
        )
        copies[-1].start()
    return copies


def pick_places(levels, tokens, first, rows):
    unit = tokens // 16
    places = []
    base = 0
    for level in range(1, levels):
        count = rows >> level
        at = base + (first >> level)
        lows = [
            at,
            at - 8 * unit if level == 2 else None,
            at - 12 * unit if level >= 3 else None,
            at - 14 * unit if level == 4 else None,
        ]
        places.append((count, lows))
        base += tokens >> level
    return places


def project_kernel(where, n_arrays, first, heads, levels, q_scale, has_before, final, n_old, *refs):
    owner_ref, offset_ref = refs[:2]
    arrays = refs[2 : 2 + n_arrays]
    gain_ref, *w_refs = refs[2 + n_arrays : 6 + n_arrays]
    refs = refs[6 + n_arrays :]
    if has_before:
        acc_in, square_in = refs[:2]
        refs = refs[2:]
    refs = refs[n_old:]
    n_out = 7 if final else 2
    outs, refs = refs[:n_out], refs[n_out:]
    x_s, w_s, acc_s, square_s, piece_sems, w_sems, acc_sems, square_sem = refs[:8]
    rows = x_s.shape[0]
    depth = x_s.shape[1] // len(where)

    copies = copy_pieces(where, owner_ref, arrays, x_s, piece_sems, False)
    w_copies = []
    for i, w_ref in enumerate(w_refs):
        for number in range(len(where)):
            low = pl.multiple_of(owner_ref[number] * depth, depth)
            w_copies.append(
                pltpu.make_async_copy(
                    w_ref.at[pl.ds(low, depth)],
                    w_s.at[i, number * depth : (number + 1) * depth],
                    w_sems.at[i, number],
                )
            )
            w_copies[-1].start()
    before = []
    if has_before:
        square_copy = pltpu.make_async_copy(square_in, square_s, square_sem)
        square_copy.start()
        before = [pltpu.make_async_copy(acc_in.at[i], acc_s.at[i], acc_sems.at[i]) for i in range(3)]
        for copy in before:
            copy.start()
        square_copy.wait()
    else:
        square_s[...] = jnp.zeros_like(square_s)

    for number, copy in enumerate(copies):
        copy.wait()
        gain = gain_ref[pl.ds(owner_ref[number], 1), :]
        lanes = slice(number * depth, (number + 1) * depth)

        def gained(i, carry, gain=gain, lanes=lanes):
            at = pl.ds(pl.multiple_of(i * 64, 64), 64)
            value = x_s[at, lanes].astype(F32)
            square = value * value
            total = square_s[at, :]
            for low in range(0, depth, 128):
                total += square[:, low : low + 128]
            square_s[at, :] = total
            x_s[at, lanes] = (value * gain).astype(BF16)
            return carry

        lax.fori_loop(0, rows // 64, gained, 0, unroll=2)

    tile = 256
    waits = []
    if final:
        kvq_s, split_s, pick_s, out_sems, pick_sems = refs[8:]
        k_out, v_out, q_out = outs[:3]
        picks = outs[3:7]
    for i in range(3):
        for copy in w_copies[len(where) * i : len(where) * (i + 1)] + before[i : i + 1]:
            copy.wait()

        @pl.loop(0, rows // tile)
        def _(n, i=i):
            at = pl.ds(pl.multiple_of(n * tile, tile), tile)
            full = jnp.dot(x_s[at, :], w_s[i], preferred_element_type=F32)
            if has_before:
                full += acc_s[i, at, :]
            if not final:
                acc_s[i, at, :] = full
                return
            mean = jnp.sum(square_s[at, :], 1, keepdims=True) / (depth * 8)
            scaled = lax.rsqrt(mean + 1e-05)
            full = full * (scaled * q_scale if i == 2 else scaled)
            kvq_s[i, at, :] = full.astype(BF16)
            if i < 2:
                for head in range(heads):
                    split_s[i * heads + head, at, :] = full[:, head * 128 : head * 128 + 128]

        if final:
            out = (k_out, v_out, q_out)[i]
            here = slice(first, first + rows)
            waits.append(pltpu.make_async_copy(kvq_s.at[i], out.at[here], out_sems.at[i]))
        else:
            waits.append(pltpu.make_async_copy(acc_s.at[i], outs[0].at[i], acc_sems.at[i]))
        waits[-1].start()
        if i != 1 or not final:
            continue
        tokens = k_out.shape[0]
        local = 0
        for level, (count, lows) in enumerate(pick_places(levels, tokens, first, rows), 1):
            for head in range(heads):
                start = offset_ref[level, head]
                for side in range(2):
                    lane = (side * heads + head) * 128
                    pick_s[local : local + count, lane : lane + 128] = split_s[
                        side * heads + head, pl.ds(start, count, stride=2**level), :
                    ].astype(BF16)
            for which, low in enumerate(lows):
                if low is not None:
                    waits.append(
                        pltpu.make_async_copy(
                            pick_s.at[local : local + count],
                            picks[which].at[low : low + count],
                            pick_sems.at[level - 1, which],
                        )
                    )
                    waits[-1].start()
            local += count
    if not final:
        waits.append(pltpu.make_async_copy(square_s, outs[1], square_sem))
        waits[-1].start()
    for copy in waits:
        copy.wait()


def project(pieces, first, tokens, before, old, final, norm_gain, weights, offsets, us):
    operands, where = split_pieces(pieces)
    rows, depth = pieces[-1][0].shape[-2:]
    width = weights[0].shape[1]
    levels, heads = offsets.shape
    unit = tokens // 16
    if final:
        outs = [jax.ShapeDtypeStruct((tokens, width), BF16)] * 3
        outs += [jax.ShapeDtypeStruct((n * unit, 2 * width), BF16) for n in (15, 4, 3, 1)]
    else:
        outs = [
            jax.ShapeDtypeStruct((3, rows, width), F32),
            jax.ShapeDtypeStruct((rows, 128), F32),
        ]
    anywhere = pl.BlockSpec(memory_space=pl.ANY)
    scalars = pl.BlockSpec(memory_space=pltpu.SMEM)
    vector = pl.BlockSpec(memory_space=pltpu.VMEM)
    scratch = [
        pltpu.VMEM((rows, len(where) * depth), BF16),
        pltpu.VMEM((3, len(where) * depth, width), BF16),
        pltpu.VMEM((3, rows, width) if before or not final else (1, 8, 128), F32),
        pltpu.VMEM((rows, 128), F32),
        pltpu.SemaphoreType.DMA((len(where),)),
        pltpu.SemaphoreType.DMA((3, len(where))),
        pltpu.SemaphoreType.DMA((3,)),
        pltpu.SemaphoreType.DMA,
    ]
    if final:
        scratch += [
            pltpu.VMEM((3, rows, width), BF16),
            pltpu.VMEM((2 * heads, rows, 128), F32),
            pltpu.VMEM((rows * 15 // 16, 2 * width), BF16),
            pltpu.SemaphoreType.DMA((3,)),
            pltpu.SemaphoreType.DMA((levels - 1, 4)),
        ]
    lead = 6 + len(operands) + len(before)
    return pl.pallas_call(
        functools.partial(
            project_kernel,
            where,
            len(operands),
            first,
            heads,
            levels,
            LOG2E * (width // heads) ** (-0.5),
            bool(before),
            final,
            len(old),
        ),
        in_specs=[scalars, scalars]
        + [anywhere] * len(operands)
        + [vector]
        + [anywhere] * (3 + len(before) + len(old)),
        out_specs=[anywhere for _ in outs],
        scratch_shapes=scratch,
        out_shape=outs,
        input_output_aliases={lead + i: i for i in range(len(old))},
        compiler_params=pltpu.CompilerParams(vmem_limit_bytes=VMEM_LIMIT),
        cost_estimate=cost(us),
        name="project",
    )(
        piece_owners(pieces),
        offsets,
        *operands,
        norm_gain.reshape(-1, depth),
        *weights,
        *before,
        *old,
    )


def first_exchange(own, second, p34, fourth):
    by_x = seq_swap(p34, 2)
    by_y = seq_swap(p34, 4)
    by_x2 = seq_swap(second, 2)
    by_y2 = seq_swap(fourth, 8)
    by_y3 = seq_swap(fourth, 12)
    core_own = seq_swap(own, 1)
    return own, core_own, by_x, by_y, by_x2, by_y2, by_y3


def second_exchange(own, core_own, by_x, by_y, by_x2, by_y2, by_y3, ready):
    unit = by_y2.shape[0]
    by_x, by_y, by_x2 = after(by_x, ready, by_y), after(by_y, ready), after(by_x2, ready)
    by_y2, by_y3 = after(by_y2, ready), after(by_y3, ready)
    by_yx = seq_swap(by_x, 4)
    x_fourth = by_x[2 * unit :]
    by_y2x = seq_swap(x_fourth, 8)
    by_y3x = seq_swap(x_fourth, 12)
    others = [by_x, by_y, by_x2, by_y2, by_y3, by_yx, by_y2x, by_y3x]
    return own, core_own, *others, *[seq_swap(value, 1) for value in others]


def level_blocks(level, unit):
    count = unit * (16 >> level)
    base = unit * (0, 0, 8, 12, 14)[level]
    blocks = [(0, base, count, 0), (1, base, count, 1)]
    other = []
    if level == 2:
        other.append((4, 0, 2))
    if level >= 3:
        other += [(n, (0, 2)[level - 3], m) for n, m in ((2, 2), (3, 4), (7, 6))]
    if level == 4:
        other += [(5, 0, 8), (6, 0, 12), (8, 0, 10), (9, 0, 14)]
    for source, low, mask in other:
        blocks += [(source, low * unit, count, mask), (source + 8, low * unit, count, mask + 1)]
    return blocks


def key_table(unit, levels):
    position = lax.axis_index("seq")
    rows = []
    for level in range(1, levels):
        columns = []
        for _, _, count, mask in level_blocks(level, unit):
            if mask == 0:
                columns.append(jnp.arange(count, dtype=jnp.int32))
            else:
                top = 1 << (mask.bit_length() - 1)
                columns.append(jnp.full((count,), jnp.where((position & top) != 0, -1, FAR), jnp.int32))
        rows.append(jnp.concatenate(columns))
    return jnp.stack(rows)


TILE = 256
NT = (((1,), (1,)), ((), ()))


def local_kernel(q_ref, k_ref, v_ref, m_ref, l_ref, a_ref, v_s):
    tokens = q_ref.shape[0]
    v_s[:, :128] = v_ref[...]
    v_s[:, 128:] = jnp.ones((tokens, 128), BF16)
    lower = lax.broadcasted_iota(jnp.int32, (TILE, TILE), 0) >= lax.broadcasted_iota(
        jnp.int32, (TILE, TILE), 1
    )
    for number in range(tokens // TILE):
        low, high = number * TILE, number * TILE + TILE
        query = q_ref[low:high, :]
        own = lax.dot_general(query, k_ref[low:high, :], NT, preferred_element_type=F32)
        scores = jnp.where(lower, own, LOW)
        if number:
            before = lax.dot_general(query, k_ref[:low, :], NT, preferred_element_type=F32)
            scores = jnp.concatenate([before, scores], 1)
        top = jnp.max(scores, 1, keepdims=True)
        probs = jnp.exp2(scores - top).astype(BF16)
        both = jnp.dot(probs, v_s[:high, :], preferred_element_type=F32)
        m_ref[low:high, :] = jnp.broadcast_to(top, (TILE, 128))
        a_ref[low:high, :] = both[:, :128]
        l_ref[low:high, :] = both[:, 128:]


def attend_local(q, k, v):
    tokens, width = q.shape
    block = pl.BlockSpec((tokens, 128), lambda h: (0, h))
    return pl.pallas_call(
        local_kernel,
        grid=(width // 128,),
        in_specs=[block] * 3,
        out_specs=[block] * 3,
        scratch_shapes=[pltpu.VMEM((tokens, 256), BF16)],
        out_shape=[jax.ShapeDtypeStruct((tokens, width), F32)] * 3,
        compiler_params=pltpu.CompilerParams(vmem_limit_bytes=VMEM_LIMIT),
        cost_estimate=cost(9),
        name="attend_local",
    )(q, k, v)


def attend_kernel(levels, head_base, *refs):
    offset_ref, q_ref, m_ref, l_ref, a_ref = refs[:5]
    k_group, v_group = refs[5:23], refs[23:41]
    table_ref, out_ref, q_f, k_s, v_s, m_s, l_s, a_s = refs[41:]
    head = head_base + pl.program_id(0)
    tokens = q_f.shape[0]
    unit = k_group[0].shape[0] // 15
    q_f[...] = q_ref[...].astype(F32)
    m_s[...] = m_ref[...]
    l_s[...] = l_ref[...]
    a_s[...] = a_ref[...]
    v_s[:, 128:] = jnp.ones((tokens, 128), BF16)

    for level in range(1, levels):
        dilation = 2**level
        picked = tokens // dilation
        start = offset_ref[level, head]
        row = 0
        for source, low, count, _ in level_blocks(level, unit):
            k_s[row : row + count, :] = k_group[source][low : low + count, :]
            v_s[row : row + count, :128] = v_group[source][low : low + count, :]
            row += count
        order = table_ref[level - 1 : level, :]
        size = min(TILE, picked)
        for number in range(picked // size):
            rows = pl.ds(start + number * size * dilation, size, stride=dilation)
            query = q_f[rows, :].astype(BF16)
            scores = lax.dot_general(query, k_s[...], NT, preferred_element_type=F32)
            at = lax.broadcasted_iota(jnp.int32, (size, tokens), 0) + number * size
            scores = jnp.where(order <= at, scores, LOW)
            m_old = m_s[rows, :]
            top = jnp.maximum(m_old[:, :1], jnp.max(scores, 1, keepdims=True))
            probs = jnp.exp2(scores - top).astype(BF16)
            both = jnp.dot(probs, v_s[...], preferred_element_type=F32)
            factor = jnp.exp2(m_old - top)
            m_s[rows, :] = jnp.broadcast_to(top, (size, 128))
            a_s[rows, :] = factor * a_s[rows, :] + both[:, :128]
            l_s[rows, :] = factor * l_s[rows, :] + both[:, 128:]

    out_ref[...] = (a_s[...] / l_s[...]).astype(BF16)


def attend(q, state, exchanged, table, offsets, head_base):
    levels, heads = offsets.shape
    tokens = q.shape[0]
    half = heads // 2
    mine = pl.BlockSpec((tokens, 128), lambda h, offset: (0, h + head_base))

    def group_spec(array, shift):
        return pl.BlockSpec((array.shape[0], 128), lambda h, offset: (0, h + shift))

    return pl.pallas_call(
        functools.partial(attend_kernel, levels, head_base),
        grid_spec=pltpu.PrefetchScalarGridSpec(
            num_scalar_prefetch=1,
            grid=(half,),
            in_specs=[mine] * 4
            + [group_spec(a, head_base) for a in exchanged]
            + [group_spec(a, heads + head_base) for a in exchanged]
            + [whole_spec(table)],
            out_specs=pl.BlockSpec((tokens, 128), lambda h, offset: (0, h)),
            scratch_shapes=[
                pltpu.VMEM((tokens, 128), F32),
                pltpu.VMEM((tokens, 128), BF16),
                pltpu.VMEM((tokens, 256), BF16),
                pltpu.VMEM((tokens, 128), F32),
                pltpu.VMEM((tokens, 128), F32),
                pltpu.VMEM((tokens, 128), F32),
            ],
        ),
        out_shape=jax.ShapeDtypeStruct((tokens, 128 * half), BF16),
        compiler_params=pltpu.CompilerParams(vmem_limit_bytes=VMEM_LIMIT),
        cost_estimate=cost(CA),
        name="attend",
    )(offsets, q, *state, *exchanged, *exchanged, table)


def output_kernel(where, n_arrays, share, *refs):
    owner_ref, refs = refs[0], refs[1:]
    arrays, refs = refs[:n_arrays], refs[n_arrays:]
    base_ref, w_ref, out_ref, x_s, w_s, piece_sems, w_sems = refs
    copies = copy_pieces(where, owner_ref, arrays, x_s, piece_sems, True)
    for i in range(w_s.shape[1]):
        copies.append(pltpu.make_async_copy(w_ref.at[share + i], w_s.at[:, i], w_sems.at[i]))
        copies[-1].start()
    for copy in copies:
        copy.wait()
    tile = 512
    rows, depth = x_s.shape

    @pl.loop(0, rows // tile)
    def _(n):
        at = pl.ds(pl.multiple_of(n * tile, tile), tile)
        weight = w_s[...].reshape(depth, out_ref.shape[1])
        total = jnp.dot(x_s[at, :], weight, preferred_element_type=F32)
        out_ref[at, :] = (base_ref[at, :].astype(F32) + total).astype(out_ref.dtype)


def output(pieces, base, w_columns, share, dtype, us):
    operands, where = split_pieces(pieces)
    rows, width = base.shape
    shares = w_columns.shape[0] // 2
    depth = w_columns.size // width // 2
    anywhere = pl.BlockSpec(memory_space=pl.ANY)
    vector = pl.BlockSpec(memory_space=pltpu.VMEM)
    return pl.pallas_call(
        functools.partial(output_kernel, where, len(operands), share),
        in_specs=[pl.BlockSpec(memory_space=pltpu.SMEM)]
        + [anywhere] * len(operands)
        + [vector, anywhere],
        out_specs=vector,
        scratch_shapes=[
            pltpu.VMEM((rows, depth), BF16),
            pltpu.VMEM((w_columns.shape[1], shares) + w_columns.shape[2:], BF16),
            pltpu.SemaphoreType.DMA((8,)),
            pltpu.SemaphoreType.DMA((shares,)),
        ],
        out_shape=jax.ShapeDtypeStruct((rows, width), dtype),
        compiler_params=pltpu.CompilerParams(vmem_limit_bytes=VMEM_LIMIT),
        cost_estimate=cost(us),
        name="output",
    )(piece_owners(pieces), *operands, base, w_columns)


def column_shares(w_out):
    seq = lax.axis_index("seq")
    share = seq // 4 * 2 + seq % 2
    rows = w_out.shape[0] // 8
    part = lax.dynamic_slice_in_dim(w_out, share * rows, rows, 0)
    width = w_out.shape[1] // 8
    cut = part.reshape(rows, 8, width).transpose(1, 0, 2)
    return lax.all_to_all(cut, "tp", 0, 0, tiled=True)


def gather_shares(mine):
    groups = [[y * 4 + x_lo * 2 + core for y in range(4) for core in range(2)] for x_lo in range(2)]
    return lax.all_gather(mine, "seq", axis=0, axis_index_groups=groups)


def after(value, *others):
    return lax.optimization_barrier((value, *others))[0]


def on_device(tokens, norm_gain, w_query, w_key, w_value, w_out, offsets):
    rows = tokens.shape[0]
    levels, heads = offsets.shape
    low = rows // 4
    weights = (w_key, w_value, w_query)

    mine = column_shares(w_out)
    t0, t1 = tokens[:low], after(tokens[low:], mine)
    below0, above0 = z_shift(t0, 1), z_shift(t0, -1)
    other0, other1 = x_swap(t0), x_swap(t1)
    far0 = z_shift(below0, 1)
    pair1 = jnp.stack([t1, after(other1, below0, above0)])
    below1, above1 = z_shift(pair1, 1), z_shift(pair1, -1)
    others0 = x_swap(jnp.stack([below0, above0, far0]))
    first = z_first_pieces(t0, below0, above0, far0, other0, others0)
    old = project(first, 0, rows, [], [], True, norm_gain, weights, offsets, C0)
    w_columns = gather_shares(after(mine, far0))
    if F1:
        below1 = after(below1, old[1])
    far1 = z_shift(below1[0], 1), z_shift(above1[1], -1)
    second = x_first_pieces(pair1, below1, above1, *far1)
    sums = project(second[:6], low, rows, [], [], False, norm_gain, weights, offsets, C1)
    old = project(second[6:], low, rows, sums, old, True, norm_gain, weights, offsets, C2)
    k, v, q = old[:3]
    exchanged = first_exchange(*old[3:])
    state = attend_local(q, k, v)
    exchanged = second_exchange(*exchanged, state[0])
    table = key_table(rows // 16, levels)
    gathered = []
    att_a = attend(q, state, exchanged, table, offsets, 0)
    below_a, above_a, other_a = z_shift(att_a, 1), z_shift(att_a, -1), x_swap(att_a)
    if F5:
        q = after(q, att_a)
    if F6:
        q = after(q, below_a)
    att_b = attend(q, state, exchanged, table, offsets, heads // 2)
    far_a = z_shift(below_a, 1)
    other_b = x_swap(att_b)
    if F3:
        other_b = after(other_b, below_a, above_a)
    if F4:
        below_a = after(below_a, other_a)
    pair_b = jnp.stack([att_b, other_b])
    if F8:
        others_a = x_swap(jnp.stack([below_a, above_a]))
        if F9:
            far_a = after(far_a, others_a)
        other_far_a = x_swap(far_a)
    else:
        others_a, other_far_a = x_swap(jnp.stack([below_a, above_a, far_a])), None
    below_b, above_b = z_shift(pair_b, 1), z_shift(pair_b, -1)
    far_b = z_shift(below_b[0], 1), z_shift(above_b[1], -1)
    gathered = [
        z_first_pieces(att_a, below_a, above_a, far_a, other_a, others_a, other_far_a),
        x_first_pieces(pair_b, below_b, above_b, *far_b),
    ]
    if F7:
        total = output(gathered[0], tokens, w_columns, 0, F32, 8)
        return output(gathered[1], total, w_columns, 4, BF16, CO)
    total = output(gathered[1], tokens, w_columns, 4, F32, 8)
    return output(gathered[0], total, w_columns, 0, BF16, CO)


def solution(mesh):
    placed = (
        P("seq", "tp"),
        P(),
        P(None, "tp"),
        P(None, "tp"),
        P(None, "tp"),
        P("tp", None),
        P(None, "tp"),
    )
    return jax.shard_map(
        on_device, mesh=mesh, in_specs=placed, out_specs=P("seq", "tp"), check_vma=False
    )
```

```python
import functools
import math

import jax
import jax.numpy as jnp
from jax import lax
from jax.experimental import pallas as pl
from jax.experimental.pallas import tpu as pltpu
from jax.sharding import PartitionSpec as P

BF16 = jnp.bfloat16
F32 = jnp.float32
LOG2E = math.log2(math.e)
LOW = -1e30
FAR = 1 << 20
VMEM_LIMIT = 56 * 1024 * 1024
FLOPS_PER_US = 1000000000
F1 = 1
F3 = 1
F4 = 1
F7 = 1
F8 = 0
F9 = 0
CO = 30
CA = 9
C0 = 12
C1 = 20
C2 = 8
F5 = 1
F6 = 0


def cost(us):
    return pl.CostEstimate(flops=int(us * FLOPS_PER_US), bytes_accessed=1024, transcendentals=0)


def z_shift(value, step):
    pairs = [(t, ((t // 2 + step) % 4) * 2 + t % 2) for t in range(8)]
    return lax.ppermute(value, "tp", pairs)


def x_swap(value):
    return lax.ppermute(value, "tp", [(t, t ^ 1) for t in range(8)])


def seq_swap(value, mask):
    return lax.ppermute(value, "seq", [(s, s ^ mask) for s in range(16)])


def x_first_pieces(pair, below, above, far_own, far_other):
    return [
        (pair, 0, 0, 0),
        (pair, 1, 0, 1),
        (below, 0, -1, 0),
        (below, 1, -1, 1),
        (above, 0, 1, 0),
        (above, 1, 1, 1),
        (far_own, None, 2, 0),
        (far_other, None, 2, 1),
    ]


def z_first_pieces(block, below, above, far, other, others, other_far=None):
    return [
        (block, None, 0, 0),
        (below, None, -1, 0),
        (above, None, 1, 0),
        (far, None, 2, 0),
        (other, None, 0, 1),
        (others, 0, -1, 1),
        (others, 1, 1, 1),
        (others, 2, 2, 1) if other_far is None else (other_far, None, 2, 1),
    ]


def piece_owners(pieces):
    tp = lax.axis_index("tp")
    z, x = tp // 2, tp % 2
    owners = [((z + dz + 4) % 4) * 2 + (x ^ dx) for _, _, dz, dx in pieces]
    return jnp.stack(owners).astype(jnp.int32)


def split_pieces(pieces):
    arrays, where = [], []
    for array, index, _, _ in pieces:
        for number, seen in enumerate(arrays):
            if seen is array:
                break
        else:
            number = len(arrays)
            arrays.append(array)
        where.append((number, index))
    return arrays, where


def whole_spec(array):
    zeros = (0,) * array.ndim
    return pl.BlockSpec(array.shape, lambda *_: zeros)


def copy_pieces(where, owner_ref, arrays, x_s, sems, owned):
    copies = []
    for number, (array, index) in enumerate(where):
        source = arrays[array] if index is None else arrays[array].at[index]
        depth = source.shape[1]
        place = owner_ref[number] if owned else number
        low = pl.multiple_of(place * depth, depth) if owned else number * depth
        copies.append(
            pltpu.make_async_copy(source, x_s.at[:, pl.ds(low, depth)], sems.at[number])
        )
        copies[-1].start()
    return copies


def pick_places(levels, tokens, first, rows):
    unit = tokens // 16
    places = []
    base = 0
    for level in range(1, levels):
        count = rows >> level
        at = base + (first >> level)
        lows = [
            at,
            at - 8 * unit if level == 2 else None,
            at - 12 * unit if level >= 3 else None,
            at - 14 * unit if level == 4 else None,
        ]
        places.append((count, lows))
        base += tokens >> level
    return places


def project_kernel(where, n_arrays, first, heads, levels, q_scale, has_before, final, n_old, *refs):
    owner_ref, offset_ref = refs[:2]
    arrays = refs[2 : 2 + n_arrays]
    gain_ref, *w_refs = refs[2 + n_arrays : 6 + n_arrays]
    refs = refs[6 + n_arrays :]
    if has_before:
        acc_in, square_in = refs[:2]
        refs = refs[2:]
    refs = refs[n_old:]
    n_out = 7 if final else 2
    outs, refs = refs[:n_out], refs[n_out:]
    x_s, w_s, acc_s, square_s, piece_sems, w_sems, acc_sems, square_sem = refs[:8]
    rows = x_s.shape[0]
    depth = x_s.shape[1] // len(where)

    copies = copy_pieces(where, owner_ref, arrays, x_s, piece_sems, False)
    w_copies = []
    for i, w_ref in enumerate(w_refs):
        for number in range(len(where)):
            low = pl.multiple_of(owner_ref[number] * depth, depth)
            w_copies.append(
                pltpu.make_async_copy(
                    w_ref.at[pl.ds(low, depth)],
                    w_s.at[i, number * depth : (number + 1) * depth],
                    w_sems.at[i, number],
                )
            )
            w_copies[-1].start()
    before = []
    if has_before:
        square_copy = pltpu.make_async_copy(square_in, square_s, square_sem)
        square_copy.start()
        before = [pltpu.make_async_copy(acc_in.at[i], acc_s.at[i], acc_sems.at[i]) for i in range(3)]
        for copy in before:
            copy.start()
        square_copy.wait()
    else:
        square_s[...] = jnp.zeros_like(square_s)

    for number, copy in enumerate(copies):
        copy.wait()
        gain = gain_ref[pl.ds(owner_ref[number], 1), :]
        lanes = slice(number * depth, (number + 1) * depth)

        def gained(i, carry, gain=gain, lanes=lanes):
            at = pl.ds(pl.multiple_of(i * 64, 64), 64)
            value = x_s[at, lanes].astype(F32)
            square = value * value
            total = square_s[at, :]
            for low in range(0, depth, 128):
                total += square[:, low : low + 128]
            square_s[at, :] = total
            x_s[at, lanes] = (value * gain).astype(BF16)
            return carry

        lax.fori_loop(0, rows // 64, gained, 0, unroll=2)

    tile = 256
    waits = []
    if final:
        kvq_s, split_s, pick_s, out_sems, pick_sems = refs[8:]
        k_out, v_out, q_out = outs[:3]
        picks = outs[3:7]
    for i in range(3):
        for copy in w_copies[len(where) * i : len(where) * (i + 1)] + before[i : i + 1]:
            copy.wait()

        @pl.loop(0, rows // tile)
        def _(n, i=i):
            at = pl.ds(pl.multiple_of(n * tile, tile), tile)
            full = jnp.dot(x_s[at, :], w_s[i], preferred_element_type=F32)
            if has_before:
                full += acc_s[i, at, :]
            if not final:
                acc_s[i, at, :] = full
                return
            mean = jnp.sum(square_s[at, :], 1, keepdims=True) / (depth * 8)
            scaled = lax.rsqrt(mean + 1e-05)
            full = full * (scaled * q_scale if i == 2 else scaled)
            kvq_s[i, at, :] = full.astype(BF16)
            if i < 2:
                for head in range(heads):
                    split_s[i * heads + head, at, :] = full[:, head * 128 : head * 128 + 128]

        if final:
            out = (k_out, v_out, q_out)[i]
            here = slice(first, first + rows)
            waits.append(pltpu.make_async_copy(kvq_s.at[i], out.at[here], out_sems.at[i]))
        else:
            waits.append(pltpu.make_async_copy(acc_s.at[i], outs[0].at[i], acc_sems.at[i]))
        waits[-1].start()
        if i != 1 or not final:
            continue
        tokens = k_out.shape[0]
        local = 0
        for level, (count, lows) in enumerate(pick_places(levels, tokens, first, rows), 1):
            for head in range(heads):
                start = offset_ref[level, head]
                for side in range(2):
                    lane = (side * heads + head) * 128
                    pick_s[local : local + count, lane : lane + 128] = split_s[
                        side * heads + head, pl.ds(start, count, stride=2**level), :
                    ].astype(BF16)
            for which, low in enumerate(lows):
                if low is not None:
                    waits.append(
                        pltpu.make_async_copy(
                            pick_s.at[local : local + count],
                            picks[which].at[low : low + count],
                            pick_sems.at[level - 1, which],
                        )
                    )
                    waits[-1].start()
            local += count
    if not final:
        waits.append(pltpu.make_async_copy(square_s, outs[1], square_sem))
        waits[-1].start()
    for copy in waits:
        copy.wait()


def project(pieces, first, tokens, before, old, final, norm_gain, weights, offsets, us):
    operands, where = split_pieces(pieces)
    rows, depth = pieces[-1][0].shape[-2:]
    width = weights[0].shape[1]
    levels, heads = offsets.shape
    unit = tokens // 16
    if final:
        outs = [jax.ShapeDtypeStruct((tokens, width), BF16)] * 3
        outs += [jax.ShapeDtypeStruct((n * unit, 2 * width), BF16) for n in (15, 4, 3, 1)]
    else:
        outs = [
            jax.ShapeDtypeStruct((3, rows, width), F32),
            jax.ShapeDtypeStruct((rows, 128), F32),
        ]
    anywhere = pl.BlockSpec(memory_space=pl.ANY)
    scalars = pl.BlockSpec(memory_space=pltpu.SMEM)
    vector = pl.BlockSpec(memory_space=pltpu.VMEM)
    scratch = [
        pltpu.VMEM((rows, len(where) * depth), BF16),
        pltpu.VMEM((3, len(where) * depth, width), BF16),
        pltpu.VMEM((3, rows, width) if before or not final else (1, 8, 128), F32),
        pltpu.VMEM((rows, 128), F32),
        pltpu.SemaphoreType.DMA((len(where),)),
        pltpu.SemaphoreType.DMA((3, len(where))),
        pltpu.SemaphoreType.DMA((3,)),
        pltpu.SemaphoreType.DMA,
    ]
    if final:
        scratch += [
            pltpu.VMEM((3, rows, width), BF16),
            pltpu.VMEM((2 * heads, rows, 128), F32),
            pltpu.VMEM((rows * 15 // 16, 2 * width), BF16),
            pltpu.SemaphoreType.DMA((3,)),
            pltpu.SemaphoreType.DMA((levels - 1, 4)),
        ]
    lead = 6 + len(operands) + len(before)
    return pl.pallas_call(
        functools.partial(
            project_kernel,
            where,
            len(operands),
            first,
            heads,
            levels,
            LOG2E * (width // heads) ** (-0.5),
            bool(before),
            final,
            len(old),
        ),
        in_specs=[scalars, scalars]
        + [anywhere] * len(operands)
        + [vector]
        + [anywhere] * (3 + len(before) + len(old)),
        out_specs=[anywhere for _ in outs],
        scratch_shapes=scratch,
        out_shape=outs,
        input_output_aliases={lead + i: i for i in range(len(old))},
        compiler_params=pltpu.CompilerParams(vmem_limit_bytes=VMEM_LIMIT),
        cost_estimate=cost(us),
        name="project",
    )(
        piece_owners(pieces),
        offsets,
        *operands,
        norm_gain.reshape(-1, depth),
        *weights,
        *before,
        *old,
    )


def first_exchange(own, second, p34, fourth):
    by_x = seq_swap(p34, 2)
    by_y = seq_swap(p34, 4)
    by_x2 = seq_swap(second, 2)
    by_y2 = seq_swap(fourth, 8)
    by_y3 = seq_swap(fourth, 12)
    core_own = seq_swap(own, 1)
    return own, core_own, by_x, by_y, by_x2, by_y2, by_y3


def second_exchange(own, core_own, by_x, by_y, by_x2, by_y2, by_y3, ready):
    unit = by_y2.shape[0]
    by_x, by_y, by_x2 = after(by_x, ready, by_y), after(by_y, ready), after(by_x2, ready)
    by_yx = seq_swap(by_x, 4)
    x_fourth = by_x[2 * unit :]
    by_y2x = seq_swap(x_fourth, 8)
    by_y3x = seq_swap(x_fourth, 12)
    by_y2, by_y3 = after(by_y2, by_yx), after(by_y3, by_yx)
    others = [by_x, by_y, by_x2, by_y2, by_y3, by_yx, by_y2x, by_y3x]
    return own, core_own, *others, *[seq_swap(value, 1) for value in others]


def level_blocks(level, unit):
    count = unit * (16 >> level)
    base = unit * (0, 0, 8, 12, 14)[level]
    blocks = [(0, base, count, 0), (1, base, count, 1)]
    other = []
    if level == 2:
        other.append((4, 0, 2))
    if level >= 3:
        other += [(n, (0, 2)[level - 3], m) for n, m in ((2, 2), (3, 4), (7, 6))]
    if level == 4:
        other += [(5, 0, 8), (6, 0, 12), (8, 0, 10), (9, 0, 14)]
    for source, low, mask in other:
        blocks += [(source, low * unit, count, mask), (source + 8, low * unit, count, mask + 1)]
    return blocks


def key_table(unit, levels):
    position = lax.axis_index("seq")
    rows = []
    for level in range(1, levels):
        columns = []
        for _, _, count, mask in level_blocks(level, unit):
            if mask == 0:
                columns.append(jnp.arange(count, dtype=jnp.int32))
            else:
                top = 1 << (mask.bit_length() - 1)
                columns.append(jnp.full((count,), jnp.where((position & top) != 0, -1, FAR), jnp.int32))
        rows.append(jnp.concatenate(columns))
    return jnp.stack(rows)


TILE = 256
NT = (((1,), (1,)), ((), ()))


def local_kernel(q_ref, k_ref, v_ref, m_ref, l_ref, a_ref, v_s):
    tokens = q_ref.shape[0]
    v_s[:, :128] = v_ref[...]
    v_s[:, 128:] = jnp.ones((tokens, 128), BF16)
    lower = lax.broadcasted_iota(jnp.int32, (TILE, TILE), 0) >= lax.broadcasted_iota(
        jnp.int32, (TILE, TILE), 1
    )
    for number in range(tokens // TILE):
        low, high = number * TILE, number * TILE + TILE
        query = q_ref[low:high, :]
        own = lax.dot_general(query, k_ref[low:high, :], NT, preferred_element_type=F32)
        scores = jnp.where(lower, own, LOW)
        if number:
            before = lax.dot_general(query, k_ref[:low, :], NT, preferred_element_type=F32)
            scores = jnp.concatenate([before, scores], 1)
        top = jnp.max(scores, 1, keepdims=True)
        probs = jnp.exp2(scores - top).astype(BF16)
        both = jnp.dot(probs, v_s[:high, :], preferred_element_type=F32)
        m_ref[low:high, :] = jnp.broadcast_to(top, (TILE, 128))
        a_ref[low:high, :] = both[:, :128]
        l_ref[low:high, :] = both[:, 128:]


def attend_local(q, k, v):
    tokens, width = q.shape
    block = pl.BlockSpec((tokens, 128), lambda h: (0, h))
    return pl.pallas_call(
        local_kernel,
        grid=(width // 128,),
        in_specs=[block] * 3,
        out_specs=[block] * 3,
        scratch_shapes=[pltpu.VMEM((tokens, 256), BF16)],
        out_shape=[jax.ShapeDtypeStruct((tokens, width), F32)] * 3,
        compiler_params=pltpu.CompilerParams(vmem_limit_bytes=VMEM_LIMIT),
        cost_estimate=cost(9),
        name="attend_local",
    )(q, k, v)


def attend_kernel(levels, head_base, *refs):
    offset_ref, q_ref, m_ref, l_ref, a_ref = refs[:5]
    k_group, v_group = refs[5:23], refs[23:41]
    table_ref, out_ref, q_f, k_s, v_s, m_s, l_s, a_s = refs[41:]
    head = head_base + pl.program_id(0)
    tokens = q_f.shape[0]
    unit = k_group[0].shape[0] // 15
    q_f[...] = q_ref[...].astype(F32)
    m_s[...] = m_ref[...]
    l_s[...] = l_ref[...]
    a_s[...] = a_ref[...]
    v_s[:, 128:] = jnp.ones((tokens, 128), BF16)

    for level in range(1, levels):
        dilation = 2**level
        picked = tokens // dilation
        start = offset_ref[level, head]
        row = 0
        for source, low, count, _ in level_blocks(level, unit):
            k_s[row : row + count, :] = k_group[source][low : low + count, :]
            v_s[row : row + count, :128] = v_group[source][low : low + count, :]
            row += count
        order = table_ref[level - 1 : level, :]
        size = min(TILE, picked)
        for number in range(picked // size):
            rows = pl.ds(start + number * size * dilation, size, stride=dilation)
            query = q_f[rows, :].astype(BF16)
            scores = lax.dot_general(query, k_s[...], NT, preferred_element_type=F32)
            at = lax.broadcasted_iota(jnp.int32, (size, tokens), 0) + number * size
            scores = jnp.where(order <= at, scores, LOW)
            m_old = m_s[rows, :]
            top = jnp.maximum(m_old[:, :1], jnp.max(scores, 1, keepdims=True))
            probs = jnp.exp2(scores - top).astype(BF16)
            both = jnp.dot(probs, v_s[...], preferred_element_type=F32)
            factor = jnp.exp2(m_old - top)
            m_s[rows, :] = jnp.broadcast_to(top, (size, 128))
            a_s[rows, :] = factor * a_s[rows, :] + both[:, :128]
            l_s[rows, :] = factor * l_s[rows, :] + both[:, 128:]

    out_ref[...] = (a_s[...] / l_s[...]).astype(BF16)


def attend(q, state, exchanged, table, offsets, head_base):
    levels, heads = offsets.shape
    tokens = q.shape[0]
    half = heads // 2
    mine = pl.BlockSpec((tokens, 128), lambda h, offset: (0, h + head_base))

    def group_spec(array, shift):
        return pl.BlockSpec((array.shape[0], 128), lambda h, offset: (0, h + shift))

    return pl.pallas_call(
        functools.partial(attend_kernel, levels, head_base),
        grid_spec=pltpu.PrefetchScalarGridSpec(
            num_scalar_prefetch=1,
            grid=(half,),
            in_specs=[mine] * 4
            + [group_spec(a, head_base) for a in exchanged]
            + [group_spec(a, heads + head_base) for a in exchanged]
            + [whole_spec(table)],
            out_specs=pl.BlockSpec((tokens, 128), lambda h, offset: (0, h)),
            scratch_shapes=[
                pltpu.VMEM((tokens, 128), F32),
                pltpu.VMEM((tokens, 128), BF16),
                pltpu.VMEM((tokens, 256), BF16),
                pltpu.VMEM((tokens, 128), F32),
                pltpu.VMEM((tokens, 128), F32),
                pltpu.VMEM((tokens, 128), F32),
            ],
        ),
        out_shape=jax.ShapeDtypeStruct((tokens, 128 * half), BF16),
        compiler_params=pltpu.CompilerParams(vmem_limit_bytes=VMEM_LIMIT),
        cost_estimate=cost(CA),
        name="attend",
    )(offsets, q, *state, *exchanged, *exchanged, table)


def output_kernel(where, n_arrays, share, *refs):
    owner_ref, refs = refs[0], refs[1:]
    arrays, refs = refs[:n_arrays], refs[n_arrays:]
    base_ref, w_ref, out_ref, x_s, w_s, piece_sems, w_sems = refs
    copies = copy_pieces(where, owner_ref, arrays, x_s, piece_sems, True)
    for i in range(w_s.shape[1]):
        copies.append(pltpu.make_async_copy(w_ref.at[share + i], w_s.at[:, i], w_sems.at[i]))
        copies[-1].start()
    for copy in copies:
        copy.wait()
    tile = 512
    rows, depth = x_s.shape

    @pl.loop(0, rows // tile)
    def _(n):
        at = pl.ds(pl.multiple_of(n * tile, tile), tile)
        weight = w_s[...].reshape(depth, out_ref.shape[1])
        total = jnp.dot(x_s[at, :], weight, preferred_element_type=F32)
        out_ref[at, :] = (base_ref[at, :].astype(F32) + total).astype(out_ref.dtype)


def output(pieces, base, w_columns, share, dtype, us):
    operands, where = split_pieces(pieces)
    rows, width = base.shape
    shares = w_columns.shape[0] // 2
    depth = w_columns.size // width // 2
    anywhere = pl.BlockSpec(memory_space=pl.ANY)
    vector = pl.BlockSpec(memory_space=pltpu.VMEM)
    return pl.pallas_call(
        functools.partial(output_kernel, where, len(operands), share),
        in_specs=[pl.BlockSpec(memory_space=pltpu.SMEM)]
        + [anywhere] * len(operands)
        + [vector, anywhere],
        out_specs=vector,
        scratch_shapes=[
            pltpu.VMEM((rows, depth), BF16),
            pltpu.VMEM((w_columns.shape[1], shares) + w_columns.shape[2:], BF16),
            pltpu.SemaphoreType.DMA((8,)),
            pltpu.SemaphoreType.DMA((shares,)),
        ],
        out_shape=jax.ShapeDtypeStruct((rows, width), dtype),
        compiler_params=pltpu.CompilerParams(vmem_limit_bytes=VMEM_LIMIT),
        cost_estimate=cost(us),
        name="output",
    )(piece_owners(pieces), *operands, base, w_columns)


def column_shares(w_out):
    seq = lax.axis_index("seq")
    share = seq // 4 * 2 + seq % 2
    rows = w_out.shape[0] // 8
    part = lax.dynamic_slice_in_dim(w_out, share * rows, rows, 0)
    width = w_out.shape[1] // 8
    cut = part.reshape(rows, 8, width).transpose(1, 0, 2)
    return lax.all_to_all(cut, "tp", 0, 0, tiled=True)


def gather_shares(mine):
    groups = [[y * 4 + x_lo * 2 + core for y in range(4) for core in range(2)] for x_lo in range(2)]
    return lax.all_gather(mine, "seq", axis=0, axis_index_groups=groups)


def after(value, *others):
    return lax.optimization_barrier((value, *others))[0]


def on_device(tokens, norm_gain, w_query, w_key, w_value, w_out, offsets):
    rows = tokens.shape[0]
    levels, heads = offsets.shape
    low = rows // 4
    weights = (w_key, w_value, w_query)

    t0, t1 = tokens[:low], tokens[low:]
    below0, above0 = z_shift(t0, 1), z_shift(t0, -1)
    other0, other1 = x_swap(t0), x_swap(t1)
    far0 = z_shift(below0, 1)
    pair1 = jnp.stack([t1, after(other1, below0, above0, far0)])
    below1, above1 = z_shift(pair1, 1), z_shift(pair1, -1)
    others0 = x_swap(jnp.stack([below0, above0, far0]))
    first = z_first_pieces(t0, below0, above0, far0, other0, others0)
    old = project(first, 0, rows, [], [], True, norm_gain, weights, offsets, C0)
    if F1:
        below1 = after(below1, old[1])
    far1 = z_shift(below1[0], 1), z_shift(above1[1], -1)
    mine = column_shares(after(w_out, far0))
    second = x_first_pieces(pair1, after(below1, mine), above1, *far1)
    sums = project(second[:6], low, rows, [], [], False, norm_gain, weights, offsets, C1)
    w_columns = gather_shares(after(mine, sums[1]))
    old = project(second[6:], low, rows, sums, old, True, norm_gain, weights, offsets, C2)
    k, v, q = old[:3]
    exchanged = first_exchange(*old[3:])
    state = attend_local(q, k, v)
    exchanged = second_exchange(*exchanged, state[0])
    table = key_table(rows // 16, levels)
    gathered = []
    att_a = attend(q, state, exchanged, table, offsets, 0)
    below_a, above_a, other_a = z_shift(att_a, 1), z_shift(att_a, -1), x_swap(att_a)
    if F5:
        q = after(q, att_a)
    if F6:
        q = after(q, below_a)
    att_b = attend(q, state, exchanged, table, offsets, heads // 2)
    far_a = z_shift(below_a, 1)
    other_b = x_swap(att_b)
    if F3:
        other_b = after(other_b, below_a, above_a)
    if F4:
        below_a = after(below_a, other_a)
    pair_b = jnp.stack([att_b, other_b])
    if F8:
        others_a = x_swap(jnp.stack([below_a, above_a]))
        if F9:
            far_a = after(far_a, others_a)
        other_far_a = x_swap(far_a)
    else:
        others_a, other_far_a = x_swap(jnp.stack([below_a, above_a, far_a])), None
    below_b, above_b = z_shift(pair_b, 1), z_shift(pair_b, -1)
    far_b = z_shift(below_b[0], 1), z_shift(above_b[1], -1)
    gathered = [
        z_first_pieces(att_a, below_a, above_a, far_a, other_a, others_a, other_far_a),
        x_first_pieces(pair_b, below_b, above_b, *far_b),
    ]
    if F7:
        total = output(gathered[0], tokens, w_columns, 0, F32, 8)
        return output(gathered[1], total, w_columns, 4, BF16, CO)
    total = output(gathered[1], tokens, w_columns, 4, F32, 8)
    return output(gathered[0], total, w_columns, 0, BF16, CO)


def solution(mesh):
    placed = (
        P("seq", "tp"),
        P(),
        P(None, "tp"),
        P(None, "tp"),
        P(None, "tp"),
        P("tp", None),
        P(None, "tp"),
    )
    return jax.shard_map(
        on_device, mesh=mesh, in_specs=placed, out_specs=P("seq", "tp"), check_vma=False
    )
```

```python
import functools
import math

import jax
import jax.numpy as jnp
from jax import lax
from jax.experimental import pallas as pl
from jax.experimental.pallas import tpu as pltpu
from jax.sharding import PartitionSpec as P

BF16 = jnp.bfloat16
F32 = jnp.float32
LOG2E = math.log2(math.e)
LOW = -1e30
FAR = 1 << 20
VMEM_LIMIT = 56 * 1024 * 1024
FLOPS_PER_US = 1000000000
F1 = 1
F3 = 1
F4 = 1
F7 = 1
F8 = 0
F9 = 0
CO = 30
CX = 0.01
CA = 9
C0 = 12
C1 = 20
C2 = 8
F5 = 1


def cost(us):
    return pl.CostEstimate(flops=int(us * FLOPS_PER_US), bytes_accessed=1024, transcendentals=0)


def z_shift(value, step):
    pairs = [(t, ((t // 2 + step) % 4) * 2 + t % 2) for t in range(8)]
    return lax.ppermute(value, "tp", pairs)


def x_swap(value):
    return lax.ppermute(value, "tp", [(t, t ^ 1) for t in range(8)])


def seq_swap(value, mask):
    return lax.ppermute(value, "seq", [(s, s ^ mask) for s in range(16)])


def x_first_pieces(pair, below, above, far_own, far_other):
    return [
        (pair, 0, 0, 0),
        (pair, 1, 0, 1),
        (below, 0, -1, 0),
        (below, 1, -1, 1),
        (above, 0, 1, 0),
        (above, 1, 1, 1),
        (far_own, None, 2, 0),
        (far_other, None, 2, 1),
    ]


def z_first_pieces(block, below, above, far, other, others, other_far=None):
    return [
        (block, None, 0, 0),
        (below, None, -1, 0),
        (above, None, 1, 0),
        (far, None, 2, 0),
        (other, None, 0, 1),
        (others, 0, -1, 1),
        (others, 1, 1, 1),
        (others, 2, 2, 1) if other_far is None else (other_far, None, 2, 1),
    ]


def piece_owners(pieces):
    tp = lax.axis_index("tp")
    z, x = tp // 2, tp % 2
    owners = [((z + dz + 4) % 4) * 2 + (x ^ dx) for _, _, dz, dx in pieces]
    return jnp.stack(owners).astype(jnp.int32)


def split_pieces(pieces):
    arrays, where = [], []
    for array, index, _, _ in pieces:
        for number, seen in enumerate(arrays):
            if seen is array:
                break
        else:
            number = len(arrays)
            arrays.append(array)
        where.append((number, index))
    return arrays, where


def whole_spec(array):
    zeros = (0,) * array.ndim
    return pl.BlockSpec(array.shape, lambda *_: zeros)


def copy_pieces(where, arrays, x_s, sems):
    copies = []
    for number, (array, index) in enumerate(where):
        source = arrays[array] if index is None else arrays[array].at[index]
        depth = source.shape[1]
        low = number * depth
        copies.append(
            pltpu.make_async_copy(source, x_s.at[:, pl.ds(low, depth)], sems.at[number])
        )
        copies[-1].start()
    return copies


def pick_places(levels, tokens, first, rows):
    unit = tokens // 16
    places = []
    base = 0
    for level in range(1, levels):
        count = rows >> level
        at = base + (first >> level)
        lows = [
            at,
            at - 8 * unit if level == 2 else None,
            at - 12 * unit if level >= 3 else None,
            at - 14 * unit if level == 4 else None,
        ]
        places.append((count, lows))
        base += tokens >> level
    return places


def project_kernel(where, n_arrays, first, heads, levels, q_scale, has_before, final, n_old, *refs):
    owner_ref, offset_ref = refs[:2]
    arrays = refs[2 : 2 + n_arrays]
    gain_ref, *w_refs = refs[2 + n_arrays : 6 + n_arrays]
    refs = refs[6 + n_arrays :]
    if has_before:
        acc_in, square_in = refs[:2]
        refs = refs[2:]
    refs = refs[n_old:]
    n_out = 7 if final else 2
    outs, refs = refs[:n_out], refs[n_out:]
    x_s, w_s, acc_s, square_s, piece_sems, w_sems, acc_sems, square_sem = refs[:8]
    rows = x_s.shape[0]
    depth = x_s.shape[1] // len(where)

    copies = copy_pieces(where, arrays, x_s, piece_sems)
    w_copies = []
    for i, w_ref in enumerate(w_refs):
        for number in range(len(where)):
            low = pl.multiple_of(owner_ref[number] * depth, depth)
            w_copies.append(
                pltpu.make_async_copy(
                    w_ref.at[pl.ds(low, depth)],
                    w_s.at[i, number * depth : (number + 1) * depth],
                    w_sems.at[i, number],
                )
            )
            w_copies[-1].start()
    before = []
    if has_before:
        square_copy = pltpu.make_async_copy(square_in, square_s, square_sem)
        square_copy.start()
        before = [pltpu.make_async_copy(acc_in.at[i], acc_s.at[i], acc_sems.at[i]) for i in range(3)]
        for copy in before:
            copy.start()
        square_copy.wait()
    else:
        square_s[...] = jnp.zeros_like(square_s)

    for number, copy in enumerate(copies):
        copy.wait()
        gain = gain_ref[pl.ds(owner_ref[number], 1), :]
        lanes = slice(number * depth, (number + 1) * depth)

        def gained(i, carry, gain=gain, lanes=lanes):
            at = pl.ds(pl.multiple_of(i * 64, 64), 64)
            value = x_s[at, lanes].astype(F32)
            square = value * value
            total = square_s[at, :]
            for low in range(0, depth, 128):
                total += square[:, low : low + 128]
            square_s[at, :] = total
            x_s[at, lanes] = (value * gain).astype(BF16)
            return carry

        lax.fori_loop(0, rows // 64, gained, 0, unroll=2)

    tile = 256
    waits = []
    if final:
        kvq_s, split_s, pick_s, out_sems, pick_sems = refs[8:]
        k_out, v_out, q_out = outs[:3]
        picks = outs[3:7]
    for i in range(3):
        for copy in w_copies[len(where) * i : len(where) * (i + 1)] + before[i : i + 1]:
            copy.wait()

        @pl.loop(0, rows // tile)
        def _(n, i=i):
            at = pl.ds(pl.multiple_of(n * tile, tile), tile)
            full = jnp.dot(x_s[at, :], w_s[i], preferred_element_type=F32)
            if has_before:
                full += acc_s[i, at, :]
            if not final:
                acc_s[i, at, :] = full
                return
            mean = jnp.sum(square_s[at, :], 1, keepdims=True) / (depth * 8)
            scaled = lax.rsqrt(mean + 1e-05)
            full = full * (scaled * q_scale if i == 2 else scaled)
            kvq_s[i, at, :] = full.astype(BF16)
            if i < 2:
                for head in range(heads):
                    split_s[i * heads + head, at, :] = full[:, head * 128 : head * 128 + 128]

        if final:
            out = (k_out, v_out, q_out)[i]
            here = slice(first, first + rows)
            waits.append(pltpu.make_async_copy(kvq_s.at[i], out.at[here], out_sems.at[i]))
        else:
            waits.append(pltpu.make_async_copy(acc_s.at[i], outs[0].at[i], acc_sems.at[i]))
        waits[-1].start()
        if i != 1 or not final:
            continue
        tokens = k_out.shape[0]
        local = 0
        for level, (count, lows) in enumerate(pick_places(levels, tokens, first, rows), 1):
            for head in range(heads):
                start = offset_ref[level, head]
                for side in range(2):
                    lane = (side * heads + head) * 128
                    pick_s[local : local + count, lane : lane + 128] = split_s[
                        side * heads + head, pl.ds(start, count, stride=2**level), :
                    ].astype(BF16)
            for which, low in enumerate(lows):
                if low is not None:
                    waits.append(
                        pltpu.make_async_copy(
                            pick_s.at[local : local + count],
                            picks[which].at[low : low + count],
                            pick_sems.at[level - 1, which],
                        )
                    )
                    waits[-1].start()
            local += count
    if not final:
        waits.append(pltpu.make_async_copy(square_s, outs[1], square_sem))
        waits[-1].start()
    for copy in waits:
        copy.wait()


def project(pieces, first, tokens, before, old, final, norm_gain, weights, offsets, us):
    operands, where = split_pieces(pieces)
    rows, depth = pieces[-1][0].shape[-2:]
    width = weights[0].shape[1]
    levels, heads = offsets.shape
    unit = tokens // 16
    if final:
        outs = [jax.ShapeDtypeStruct((tokens, width), BF16)] * 3
        outs += [jax.ShapeDtypeStruct((n * unit, 2 * width), BF16) for n in (15, 4, 3, 1)]
    else:
        outs = [
            jax.ShapeDtypeStruct((3, rows, width), F32),
            jax.ShapeDtypeStruct((rows, 128), F32),
        ]
    anywhere = pl.BlockSpec(memory_space=pl.ANY)
    scalars = pl.BlockSpec(memory_space=pltpu.SMEM)
    vector = pl.BlockSpec(memory_space=pltpu.VMEM)
    scratch = [
        pltpu.VMEM((rows, len(where) * depth), BF16),
        pltpu.VMEM((3, len(where) * depth, width), BF16),
        pltpu.VMEM((3, rows, width) if before or not final else (1, 8, 128), F32),
        pltpu.VMEM((rows, 128), F32),
        pltpu.SemaphoreType.DMA((len(where),)),
        pltpu.SemaphoreType.DMA((3, len(where))),
        pltpu.SemaphoreType.DMA((3,)),
        pltpu.SemaphoreType.DMA,
    ]
    if final:
        scratch += [
            pltpu.VMEM((3, rows, width), BF16),
            pltpu.VMEM((2 * heads, rows, 128), F32),
            pltpu.VMEM((rows * 15 // 16, 2 * width), BF16),
            pltpu.SemaphoreType.DMA((3,)),
            pltpu.SemaphoreType.DMA((levels - 1, 4)),
        ]
    lead = 6 + len(operands) + len(before)
    return pl.pallas_call(
        functools.partial(
            project_kernel,
            where,
            len(operands),
            first,
            heads,
            levels,
            LOG2E * (width // heads) ** (-0.5),
            bool(before),
            final,
            len(old),
        ),
        in_specs=[scalars, scalars]
        + [anywhere] * len(operands)
        + [vector]
        + [anywhere] * (3 + len(before) + len(old)),
        out_specs=[anywhere for _ in outs],
        scratch_shapes=scratch,
        out_shape=outs,
        input_output_aliases={lead + i: i for i in range(len(old))},
        compiler_params=pltpu.CompilerParams(vmem_limit_bytes=VMEM_LIMIT),
        cost_estimate=cost(us),
        name="project",
    )(
        piece_owners(pieces),
        offsets,
        *operands,
        norm_gain.reshape(-1, depth),
        *weights,
        *before,
        *old,
    )


def first_exchange(own, second, p34, fourth):
    by_x = seq_swap(p34, 2)
    by_y = seq_swap(p34, 4)
    by_x2 = seq_swap(second, 2)
    by_y2 = seq_swap(fourth, 8)
    by_y3 = seq_swap(fourth, 12)
    core_own = seq_swap(own, 1)
    return own, core_own, by_x, by_y, by_x2, by_y2, by_y3


def second_exchange(own, core_own, by_x, by_y, by_x2, by_y2, by_y3, ready):
    unit = by_y2.shape[0]
    by_x, by_y, by_x2 = after(by_x, ready, by_y), after(by_y, ready), after(by_x2, ready)
    by_yx = seq_swap(by_x, 4)
    x_fourth = by_x[2 * unit :]
    by_y2x = seq_swap(x_fourth, 8)
    by_y3x = seq_swap(x_fourth, 12)
    by_y2, by_y3 = after(by_y2, by_yx), after(by_y3, by_yx)
    others = [by_x, by_y, by_x2, by_y2, by_y3, by_yx, by_y2x, by_y3x]
    return own, core_own, *others, *[seq_swap(value, 1) for value in others]


def level_blocks(level, unit):
    count = unit * (16 >> level)
    base = unit * (0, 0, 8, 12, 14)[level]
    blocks = [(0, base, count, 0), (1, base, count, 1)]
    other = []
    if level == 2:
        other.append((4, 0, 2))
    if level >= 3:
        other += [(n, (0, 2)[level - 3], m) for n, m in ((2, 2), (3, 4), (7, 6))]
    if level == 4:
        other += [(5, 0, 8), (6, 0, 12), (8, 0, 10), (9, 0, 14)]
    for source, low, mask in other:
        blocks += [(source, low * unit, count, mask), (source + 8, low * unit, count, mask + 1)]
    return blocks


def key_table(unit, levels):
    position = lax.axis_index("seq")
    rows = []
    for level in range(1, levels):
        columns = []
        for _, _, count, mask in level_blocks(level, unit):
            if mask == 0:
                columns.append(jnp.arange(count, dtype=jnp.int32))
            else:
                top = 1 << (mask.bit_length() - 1)
                columns.append(jnp.full((count,), jnp.where((position & top) != 0, -1, FAR), jnp.int32))
        rows.append(jnp.concatenate(columns))
    return jnp.stack(rows)


TILE = 256
NT = (((1,), (1,)), ((), ()))


def local_kernel(q_ref, k_ref, v_ref, m_ref, l_ref, a_ref, v_s):
    tokens = q_ref.shape[0]
    v_s[:, :128] = v_ref[...]
    v_s[:, 128:] = jnp.ones((tokens, 128), BF16)
    lower = lax.broadcasted_iota(jnp.int32, (TILE, TILE), 0) >= lax.broadcasted_iota(
        jnp.int32, (TILE, TILE), 1
    )
    for number in range(tokens // TILE):
        low, high = number * TILE, number * TILE + TILE
        query = q_ref[low:high, :]
        own = lax.dot_general(query, k_ref[low:high, :], NT, preferred_element_type=F32)
        scores = jnp.where(lower, own, LOW)
        if number:
            before = lax.dot_general(query, k_ref[:low, :], NT, preferred_element_type=F32)
            scores = jnp.concatenate([before, scores], 1)
        top = jnp.max(scores, 1, keepdims=True)
        probs = jnp.exp2(scores - top).astype(BF16)
        both = jnp.dot(probs, v_s[:high, :], preferred_element_type=F32)
        m_ref[low:high, :] = jnp.broadcast_to(top, (TILE, 128))
        a_ref[low:high, :] = both[:, :128]
        l_ref[low:high, :] = both[:, 128:]


def attend_local(q, k, v):
    tokens, width = q.shape
    block = pl.BlockSpec((tokens, 128), lambda h: (0, h))
    return pl.pallas_call(
        local_kernel,
        grid=(width // 128,),
        in_specs=[block] * 3,
        out_specs=[block] * 3,
        scratch_shapes=[pltpu.VMEM((tokens, 256), BF16)],
        out_shape=[jax.ShapeDtypeStruct((tokens, width), F32)] * 3,
        compiler_params=pltpu.CompilerParams(vmem_limit_bytes=VMEM_LIMIT),
        cost_estimate=cost(9),
        name="attend_local",
    )(q, k, v)


def attend_kernel(levels, head_base, *refs):
    offset_ref, q_ref, m_ref, l_ref, a_ref = refs[:5]
    k_group, v_group = refs[5:23], refs[23:41]
    table_ref, out_ref, q_f, k_s, v_s, m_s, l_s, a_s = refs[41:]
    head = head_base + pl.program_id(0)
    tokens = q_f.shape[0]
    unit = k_group[0].shape[0] // 15
    q_f[...] = q_ref[...].astype(F32)
    m_s[...] = m_ref[...]
    l_s[...] = l_ref[...]
    a_s[...] = a_ref[...]
    for level in range(1, levels):
        row = 0
        for source, low, count, _ in level_blocks(level, unit):
            k_s[level - 1, row : row + count, :] = k_group[source][low : low + count, :]
            v_s[level - 1, row : row + count, :128] = v_group[source][low : low + count, :]
            row += count
        v_s[level - 1, :, 128:] = jnp.ones((tokens, 128), BF16)

    for level in range(1, levels):
        dilation = 2**level
        picked = tokens // dilation
        start = offset_ref[level, head]
        order = table_ref[level - 1 : level, :]
        size = min(TILE, picked)
        for number in range(picked // size):
            rows = pl.ds(start + number * size * dilation, size, stride=dilation)
            query = q_f[rows, :].astype(BF16)
            scores = lax.dot_general(query, k_s[level - 1], NT, preferred_element_type=F32)
            at = lax.broadcasted_iota(jnp.int32, (size, tokens), 0) + number * size
            scores = jnp.where(order <= at, scores, LOW)
            m_old = m_s[rows, :]
            top = jnp.maximum(m_old[:, :1], jnp.max(scores, 1, keepdims=True))
            probs = jnp.exp2(scores - top).astype(BF16)
            both = jnp.dot(probs, v_s[level - 1], preferred_element_type=F32)
            factor = jnp.exp2(m_old - top)
            m_s[rows, :] = jnp.broadcast_to(top, (size, 128))
            a_s[rows, :] = factor * a_s[rows, :] + both[:, :128]
            l_s[rows, :] = factor * l_s[rows, :] + both[:, 128:]

    out_ref[...] = (a_s[...] / l_s[...]).astype(BF16)


def attend(q, state, exchanged, table, offsets, head_base):
    levels, heads = offsets.shape
    tokens = q.shape[0]
    half = heads // 2
    mine = pl.BlockSpec((tokens, 128), lambda h, offset: (0, h + head_base))

    def group_spec(array, shift):
        return pl.BlockSpec((array.shape[0], 128), lambda h, offset: (0, h + shift))

    return pl.pallas_call(
        functools.partial(attend_kernel, levels, head_base),
        grid_spec=pltpu.PrefetchScalarGridSpec(
            num_scalar_prefetch=1,
            grid=(half,),
            in_specs=[mine] * 4
            + [group_spec(a, head_base) for a in exchanged]
            + [group_spec(a, heads + head_base) for a in exchanged]
            + [whole_spec(table)],
            out_specs=pl.BlockSpec((tokens, 128), lambda h, offset: (0, h)),
            scratch_shapes=[
                pltpu.VMEM((tokens, 128), F32),
                pltpu.VMEM((levels - 1, tokens, 128), BF16),
                pltpu.VMEM((levels - 1, tokens, 256), BF16),
                pltpu.VMEM((tokens, 128), F32),
                pltpu.VMEM((tokens, 128), F32),
                pltpu.VMEM((tokens, 128), F32),
            ],
        ),
        out_shape=jax.ShapeDtypeStruct((tokens, 128 * half), BF16),
        compiler_params=pltpu.CompilerParams(vmem_limit_bytes=VMEM_LIMIT),
        cost_estimate=cost(CA),
        name="attend",
    )(offsets, q, *state, *exchanged, *exchanged, table)


def output_kernel(where, n_arrays, shares, *refs):
    owner_ref, refs = refs[0], refs[1:]
    arrays, refs = refs[:n_arrays], refs[n_arrays:]
    base_ref, w_ref, out_ref, x_s, w_s, piece_sems, w_sems = refs
    copies = copy_pieces(where, arrays, x_s, piece_sems)
    for number, share in enumerate(shares):
        source = w_ref.at[share : share + w_s.shape[1], owner_ref[number]]
        copies.append(pltpu.make_async_copy(source, w_s.at[number], w_sems.at[number]))
        copies[-1].start()
    for copy in copies:
        copy.wait()
    tile = 512
    rows, depth = x_s.shape

    @pl.loop(0, rows // tile)
    def _(n):
        at = pl.ds(pl.multiple_of(n * tile, tile), tile)
        weight = w_s[...].reshape(depth, out_ref.shape[1])
        total = jnp.dot(x_s[at, :], weight, preferred_element_type=F32)
        out_ref[at, :] = (base_ref[at, :].astype(F32) + total).astype(out_ref.dtype)


def output(parts, base, w_columns, dtype, us):
    pieces = [piece for part, _ in parts for piece in part]
    shares = [share for part, share in parts for _ in part]
    operands, where = split_pieces(pieces)
    rows, width = base.shape
    depth = w_columns.size // width // 16
    anywhere = pl.BlockSpec(memory_space=pl.ANY)
    vector = pl.BlockSpec(memory_space=pltpu.VMEM)
    return pl.pallas_call(
        functools.partial(output_kernel, where, len(operands), shares),
        in_specs=[pl.BlockSpec(memory_space=pltpu.SMEM)]
        + [anywhere] * len(operands)
        + [vector, anywhere],
        out_specs=vector,
        scratch_shapes=[
            pltpu.VMEM((rows, len(where) * depth), BF16),
            pltpu.VMEM((len(where), w_columns.shape[0] // 2) + w_columns.shape[2:], BF16),
            pltpu.SemaphoreType.DMA((len(where),)),
            pltpu.SemaphoreType.DMA((len(where),)),
        ],
        out_shape=jax.ShapeDtypeStruct((rows, width), dtype),
        compiler_params=pltpu.CompilerParams(vmem_limit_bytes=VMEM_LIMIT),
        cost_estimate=cost(us),
        name="output",
    )(piece_owners(pieces), *operands, base, w_columns)


def column_shares(w_out):
    seq = lax.axis_index("seq")
    share = seq // 4 * 2 + seq % 2
    rows = w_out.shape[0] // 8
    part = lax.dynamic_slice_in_dim(w_out, share * rows, rows, 0)
    width = w_out.shape[1] // 8
    cut = part.reshape(rows, 8, width).transpose(1, 0, 2)
    return lax.all_to_all(cut, "tp", 0, 0, tiled=True)


def gather_shares(mine):
    groups = [[y * 4 + x_lo * 2 + core for y in range(4) for core in range(2)] for x_lo in range(2)]
    return lax.all_gather(mine, "seq", axis=0, axis_index_groups=groups)


def after(value, *others):
    return lax.optimization_barrier((value, *others))[0]


def on_device(tokens, norm_gain, w_query, w_key, w_value, w_out, offsets):
    rows = tokens.shape[0]
    levels, heads = offsets.shape
    low = rows // 4
    weights = (w_key, w_value, w_query)

    t0, t1 = tokens[:low], tokens[low:]
    below0, above0 = z_shift(t0, 1), z_shift(t0, -1)
    other0, other1 = x_swap(t0), x_swap(t1)
    far0 = z_shift(below0, 1)
    pair1 = jnp.stack([t1, after(other1, below0, above0, far0)])
    below1, above1 = z_shift(pair1, 1), z_shift(pair1, -1)
    others0 = x_swap(jnp.stack([below0, above0, far0]))
    first = z_first_pieces(t0, below0, above0, far0, other0, others0)
    old = project(first, 0, rows, [], [], True, norm_gain, weights, offsets, C0)
    if F1:
        below1 = after(below1, old[1])
    far1 = z_shift(below1[0], 1), z_shift(above1[1], -1)
    mine = column_shares(after(w_out, far0))
    second = x_first_pieces(pair1, after(below1, mine), above1, *far1)
    sums = project(second[:6], low, rows, [], [], False, norm_gain, weights, offsets, C1)
    w_columns = gather_shares(after(mine, sums[1]))
    old = project(second[6:], low, rows, sums, old, True, norm_gain, weights, offsets, C2)
    k, v, q = old[:3]
    exchanged = first_exchange(*old[3:])
    state = attend_local(q, k, v)
    exchanged = second_exchange(*exchanged, state[0])
    table = key_table(rows // 16, levels)
    gathered = []
    att_a = attend(q, state, exchanged, table, offsets, 0)
    below_a, above_a, other_a = z_shift(att_a, 1), z_shift(att_a, -1), x_swap(att_a)
    if F5:
        q = after(q, att_a)
    att_b = attend(q, state, exchanged, table, offsets, heads // 2)
    far_a = z_shift(below_a, 1)
    other_b = x_swap(att_b)
    if F3:
        other_b = after(other_b, below_a, above_a)
    if F4:
        below_a = after(below_a, other_a)
    pair_b = jnp.stack([att_b, other_b])
    if F8:
        others_a = x_swap(jnp.stack([below_a, above_a]))
        if F9:
            far_a = after(far_a, others_a)
        other_far_a = x_swap(far_a)
    else:
        others_a, other_far_a = x_swap(jnp.stack([below_a, above_a, far_a])), None
    below_b, above_b = z_shift(pair_b, 1), z_shift(pair_b, -1)
    far_b = z_shift(below_b[0], 1), z_shift(above_b[1], -1)
    gathered = [
        z_first_pieces(att_a, below_a, above_a, far_a, other_a, others_a, other_far_a),
        x_first_pieces(pair_b, below_b, above_b, *far_b),
    ]
    heads_a, heads_b = gathered
    total = output([(heads_a[:4], 0)], tokens, w_columns, F32, CX)
    total = output([(heads_b[:6], 4)], total, w_columns, F32, CX)
    return output([(heads_b[6:], 4), (heads_a[4:], 0)], total, w_columns, BF16, CO)


def solution(mesh):
    placed = (
        P("seq", "tp"),
        P(),
        P(None, "tp"),
        P(None, "tp"),
        P(None, "tp"),
        P("tp", None),
        P(None, "tp"),
    )
    return jax.shard_map(
        on_device, mesh=mesh, in_specs=placed, out_specs=P("seq", "tp"), check_vma=False
    )
```

```python
import functools
import math

import jax
import jax.numpy as jnp
from jax import lax
from jax.experimental import pallas as pl
from jax.experimental.pallas import tpu as pltpu
from jax.sharding import PartitionSpec as P

BF16 = jnp.bfloat16
F32 = jnp.float32
LOG2E = math.log2(math.e)
LOW = -1e30
FAR = 1 << 20
VMEM_LIMIT = 56 * 1024 * 1024
FLOPS_PER_US = 1000000000
F1 = 1
F3 = 1
F4 = 1
F7 = 1
F8 = 0
F9 = 0
CO = 30
CX = 0.01
CA = 9
C0 = 12
C1 = 20
C2 = 8
F5 = 1


def cost(us):
    return pl.CostEstimate(flops=int(us * FLOPS_PER_US), bytes_accessed=1024, transcendentals=0)


def z_shift(value, step):
    pairs = [(t, ((t // 2 + step) % 4) * 2 + t % 2) for t in range(8)]
    return lax.ppermute(value, "tp", pairs)


def x_swap(value):
    return lax.ppermute(value, "tp", [(t, t ^ 1) for t in range(8)])


def seq_swap(value, mask):
    return lax.ppermute(value, "seq", [(s, s ^ mask) for s in range(16)])


def x_first_pieces(pair, below, above, far_own, far_other):
    return [
        (pair, 0, 0, 0),
        (pair, 1, 0, 1),
        (below, 0, -1, 0),
        (below, 1, -1, 1),
        (above, 0, 1, 0),
        (above, 1, 1, 1),
        (far_own, None, 2, 0),
        (far_other, None, 2, 1),
    ]


def z_first_pieces(block, below, above, far, other, others, other_far=None):
    return [
        (block, None, 0, 0),
        (below, None, -1, 0),
        (above, None, 1, 0),
        (far, None, 2, 0),
        (other, None, 0, 1),
        (others, 0, -1, 1),
        (others, 1, 1, 1),
        (others, 2, 2, 1) if other_far is None else (other_far, None, 2, 1),
    ]


def piece_owners(pieces):
    tp = lax.axis_index("tp")
    z, x = tp // 2, tp % 2
    owners = [((z + dz + 4) % 4) * 2 + (x ^ dx) for _, _, dz, dx in pieces]
    return jnp.stack(owners).astype(jnp.int32)


def split_pieces(pieces):
    arrays, where = [], []
    for array, index, _, _ in pieces:
        for number, seen in enumerate(arrays):
            if seen is array:
                break
        else:
            number = len(arrays)
            arrays.append(array)
        where.append((number, index))
    return arrays, where


def whole_spec(array):
    zeros = (0,) * array.ndim
    return pl.BlockSpec(array.shape, lambda *_: zeros)


def copy_pieces(where, arrays, x_s, sems):
    copies = []
    for number, (array, index) in enumerate(where):
        source = arrays[array] if index is None else arrays[array].at[index]
        depth = source.shape[1]
        low = number * depth
        copies.append(
            pltpu.make_async_copy(source, x_s.at[:, pl.ds(low, depth)], sems.at[number])
        )
        copies[-1].start()
    return copies


def pick_places(levels, tokens, first, rows):
    unit = tokens // 16
    places = []
    base = 0
    for level in range(1, levels):
        count = rows >> level
        at = base + (first >> level)
        lows = [
            at,
            at - 8 * unit if level == 2 else None,
            at - 12 * unit if level >= 3 else None,
            at - 14 * unit if level == 4 else None,
        ]
        places.append((count, lows))
        base += tokens >> level
    return places


def project_kernel(where, n_arrays, first, heads, levels, q_scale, has_before, final, n_old, *refs):
    owner_ref, offset_ref = refs[:2]
    arrays = refs[2 : 2 + n_arrays]
    gain_ref, *w_refs = refs[2 + n_arrays : 6 + n_arrays]
    refs = refs[6 + n_arrays :]
    if has_before:
        acc_in, square_in = refs[:2]
        refs = refs[2:]
    refs = refs[n_old:]
    n_out = 7 if final else 2
    outs, refs = refs[:n_out], refs[n_out:]
    x_s, w_s, acc_s, square_s, piece_sems, w_sems, acc_sems, square_sem = refs[:8]
    rows = x_s.shape[0]
    depth = x_s.shape[1] // len(where)

    copies = copy_pieces(where, arrays, x_s, piece_sems)
    w_copies = []
    for i, w_ref in enumerate(w_refs):
        for number in range(len(where)):
            low = pl.multiple_of(owner_ref[number] * depth, depth)
            w_copies.append(
                pltpu.make_async_copy(
                    w_ref.at[pl.ds(low, depth)],
                    w_s.at[i, number * depth : (number + 1) * depth],
                    w_sems.at[i, number],
                )
            )
            w_copies[-1].start()
    before = []
    if has_before:
        square_copy = pltpu.make_async_copy(square_in, square_s, square_sem)
        square_copy.start()
        before = [pltpu.make_async_copy(acc_in.at[i], acc_s.at[i], acc_sems.at[i]) for i in range(3)]
        for copy in before:
            copy.start()
        square_copy.wait()
    else:
        square_s[...] = jnp.zeros_like(square_s)

    for number, copy in enumerate(copies):
        copy.wait()
        gain = gain_ref[pl.ds(owner_ref[number], 1), :]
        lanes = slice(number * depth, (number + 1) * depth)

        def gained(i, carry, gain=gain, lanes=lanes):
            at = pl.ds(pl.multiple_of(i * 64, 64), 64)
            value = x_s[at, lanes].astype(F32)
            square = value * value
            total = square_s[at, :]
            for low in range(0, depth, 128):
                total += square[:, low : low + 128]
            square_s[at, :] = total
            x_s[at, lanes] = (value * gain).astype(BF16)
            return carry

        lax.fori_loop(0, rows // 64, gained, 0, unroll=2)

    tile = 256
    waits = []
    if final:
        kvq_s, split_s, pick_s, out_sems, pick_sems = refs[8:]
        k_out, v_out, q_out = outs[:3]
        picks = outs[3:7]
    for i in range(3):
        for copy in w_copies[len(where) * i : len(where) * (i + 1)] + before[i : i + 1]:
            copy.wait()

        @pl.loop(0, rows // tile)
        def _(n, i=i):
            at = pl.ds(pl.multiple_of(n * tile, tile), tile)
            full = jnp.dot(x_s[at, :], w_s[i], preferred_element_type=F32)
            if has_before:
                full += acc_s[i, at, :]
            if not final:
                acc_s[i, at, :] = full
                return
            mean = jnp.sum(square_s[at, :], 1, keepdims=True) / (depth * 8)
            scaled = lax.rsqrt(mean + 1e-05)
            full = full * (scaled * q_scale if i == 2 else scaled)
            kvq_s[i, at, :] = full.astype(BF16)
            if i < 2:
                for head in range(heads):
                    split_s[i * heads + head, at, :] = full[:, head * 128 : head * 128 + 128]

        if final:
            out = (k_out, v_out, q_out)[i]
            here = slice(first, first + rows)
            waits.append(pltpu.make_async_copy(kvq_s.at[i], out.at[here], out_sems.at[i]))
        else:
            waits.append(pltpu.make_async_copy(acc_s.at[i], outs[0].at[i], acc_sems.at[i]))
        waits[-1].start()
        if i != 1 or not final:
            continue
        tokens = k_out.shape[0]
        local = 0
        for level, (count, lows) in enumerate(pick_places(levels, tokens, first, rows), 1):
            for head in range(heads):
                start = offset_ref[level, head]
                for side in range(2):
                    lane = (side * heads + head) * 128
                    pick_s[local : local + count, lane : lane + 128] = split_s[
                        side * heads + head, pl.ds(start, count, stride=2**level), :
                    ].astype(BF16)
            for which, low in enumerate(lows):
                if low is not None:
                    waits.append(
                        pltpu.make_async_copy(
                            pick_s.at[local : local + count],
                            picks[which].at[low : low + count],
                            pick_sems.at[level - 1, which],
                        )
                    )
                    waits[-1].start()
            local += count
    if not final:
        waits.append(pltpu.make_async_copy(square_s, outs[1], square_sem))
        waits[-1].start()
    for copy in waits:
        copy.wait()


def project(pieces, first, tokens, before, old, final, norm_gain, weights, offsets, us):
    operands, where = split_pieces(pieces)
    rows, depth = pieces[-1][0].shape[-2:]
    width = weights[0].shape[1]
    levels, heads = offsets.shape
    unit = tokens // 16
    if final:
        outs = [jax.ShapeDtypeStruct((tokens, width), BF16)] * 3
        outs += [jax.ShapeDtypeStruct((n * unit, 2 * width), BF16) for n in (15, 4, 3, 1)]
    else:
        outs = [
            jax.ShapeDtypeStruct((3, rows, width), F32),
            jax.ShapeDtypeStruct((rows, 128), F32),
        ]
    anywhere = pl.BlockSpec(memory_space=pl.ANY)
    scalars = pl.BlockSpec(memory_space=pltpu.SMEM)
    vector = pl.BlockSpec(memory_space=pltpu.VMEM)
    scratch = [
        pltpu.VMEM((rows, len(where) * depth), BF16),
        pltpu.VMEM((3, len(where) * depth, width), BF16),
        pltpu.VMEM((3, rows, width) if before or not final else (1, 8, 128), F32),
        pltpu.VMEM((rows, 128), F32),
        pltpu.SemaphoreType.DMA((len(where),)),
        pltpu.SemaphoreType.DMA((3, len(where))),
        pltpu.SemaphoreType.DMA((3,)),
        pltpu.SemaphoreType.DMA,
    ]
    if final:
        scratch += [
            pltpu.VMEM((3, rows, width), BF16),
            pltpu.VMEM((2 * heads, rows, 128), F32),
            pltpu.VMEM((rows * 15 // 16, 2 * width), BF16),
            pltpu.SemaphoreType.DMA((3,)),
            pltpu.SemaphoreType.DMA((levels - 1, 4)),
        ]
    lead = 6 + len(operands) + len(before)
    return pl.pallas_call(
        functools.partial(
            project_kernel,
            where,
            len(operands),
            first,
            heads,
            levels,
            LOG2E * (width // heads) ** (-0.5),
            bool(before),
            final,
            len(old),
        ),
        in_specs=[scalars, scalars]
        + [anywhere] * len(operands)
        + [vector]
        + [anywhere] * (3 + len(before) + len(old)),
        out_specs=[anywhere for _ in outs],
        scratch_shapes=scratch,
        out_shape=outs,
        input_output_aliases={lead + i: i for i in range(len(old))},
        compiler_params=pltpu.CompilerParams(vmem_limit_bytes=VMEM_LIMIT),
        cost_estimate=cost(us),
        name="project",
    )(
        piece_owners(pieces),
        offsets,
        *operands,
        norm_gain.reshape(-1, depth),
        *weights,
        *before,
        *old,
    )


def first_exchange(own, second, p34, fourth):
    by_x = seq_swap(p34, 2)
    by_y = seq_swap(p34, 4)
    by_x2 = seq_swap(second, 2)
    by_y2 = seq_swap(fourth, 8)
    by_y3 = seq_swap(fourth, 12)
    core_own = seq_swap(own, 1)
    return own, core_own, by_x, by_y, by_x2, by_y2, by_y3


def second_exchange(own, core_own, by_x, by_y, by_x2, by_y2, by_y3, ready):
    unit = by_y2.shape[0]
    by_x, by_y, by_x2 = after(by_x, ready, by_y), after(by_y, ready), after(by_x2, ready)
    by_yx = seq_swap(by_x, 4)
    x_fourth = by_x[2 * unit :]
    by_y2x = seq_swap(x_fourth, 8)
    by_y3x = seq_swap(x_fourth, 12)
    by_y2, by_y3 = after(by_y2, by_yx), after(by_y3, by_yx)
    others = [by_x, by_y, by_x2, by_y2, by_y3, by_yx, by_y2x, by_y3x]
    return own, core_own, *others, *[seq_swap(value, 1) for value in others]


def level_blocks(level, unit):
    count = unit * (16 >> level)
    base = unit * (0, 0, 8, 12, 14)[level]
    blocks = [(0, base, count, 0), (1, base, count, 1)]
    other = []
    if level == 2:
        other.append((4, 0, 2))
    if level >= 3:
        other += [(n, (0, 2)[level - 3], m) for n, m in ((2, 2), (3, 4), (7, 6))]
    if level == 4:
        other += [(5, 0, 8), (6, 0, 12), (8, 0, 10), (9, 0, 14)]
    for source, low, mask in other:
        blocks += [(source, low * unit, count, mask), (source + 8, low * unit, count, mask + 1)]
    return blocks


def key_table(unit, levels):
    position = lax.axis_index("seq")
    rows = []
    for level in range(1, levels):
        columns = []
        for _, _, count, mask in level_blocks(level, unit):
            if mask == 0:
                columns.append(jnp.arange(count, dtype=jnp.int32))
            else:
                top = 1 << (mask.bit_length() - 1)
                columns.append(jnp.full((count,), jnp.where((position & top) != 0, -1, FAR), jnp.int32))
        rows.append(jnp.concatenate(columns))
    return jnp.stack(rows)


TILE = 256
NT = (((1,), (1,)), ((), ()))


def local_kernel(q_ref, k_ref, v_ref, m_ref, l_ref, a_ref, v_s):
    tokens = q_ref.shape[0]
    v_s[:, :128] = v_ref[...]
    v_s[:, 128:] = jnp.ones((tokens, 128), BF16)
    lower = lax.broadcasted_iota(jnp.int32, (TILE, TILE), 0) >= lax.broadcasted_iota(
        jnp.int32, (TILE, TILE), 1
    )
    for number in range(tokens // TILE):
        low, high = number * TILE, number * TILE + TILE
        query = q_ref[low:high, :]
        own = lax.dot_general(query, k_ref[low:high, :], NT, preferred_element_type=F32)
        scores = jnp.where(lower, own, LOW)
        if number:
            before = lax.dot_general(query, k_ref[:low, :], NT, preferred_element_type=F32)
            scores = jnp.concatenate([before, scores], 1)
        top = jnp.max(scores, 1, keepdims=True)
        probs = jnp.exp2(scores - top).astype(BF16)
        both = jnp.dot(probs, v_s[:high, :], preferred_element_type=F32)
        m_ref[low:high, :] = jnp.broadcast_to(top, (TILE, 128))
        a_ref[low:high, :] = both[:, :128]
        l_ref[low:high, :] = both[:, 128:]


def attend_local(q, k, v):
    tokens, width = q.shape
    block = pl.BlockSpec((tokens, 128), lambda h: (0, h))
    return pl.pallas_call(
        local_kernel,
        grid=(width // 128,),
        in_specs=[block] * 3,
        out_specs=[block] * 3,
        scratch_shapes=[pltpu.VMEM((tokens, 256), BF16)],
        out_shape=[jax.ShapeDtypeStruct((tokens, width), F32)] * 3,
        compiler_params=pltpu.CompilerParams(vmem_limit_bytes=VMEM_LIMIT),
        cost_estimate=cost(9),
        name="attend_local",
    )(q, k, v)


def attend_kernel(levels, head_base, *refs):
    offset_ref, q_ref, m_ref, l_ref, a_ref = refs[:5]
    k_group, v_group = refs[5:23], refs[23:41]
    table_ref, out_ref, q_f, k_s, v_s, m_s, l_s, a_s = refs[41:]
    head = head_base + pl.program_id(0)
    tokens = q_f.shape[0]
    unit = k_group[0].shape[0] // 15
    q_f[...] = q_ref[...].astype(F32)
    m_s[...] = m_ref[...]
    l_s[...] = l_ref[...]
    a_s[...] = a_ref[...]
    for level in range(1, levels):
        row = 0
        for source, low, count, _ in level_blocks(level, unit):
            k_s[level - 1, row : row + count, :] = k_group[source][low : low + count, :]
            v_s[level - 1, row : row + count, :128] = v_group[source][low : low + count, :]
            row += count
        v_s[level - 1, :, 128:] = jnp.ones((tokens, 128), BF16)

    for level in range(1, levels):
        dilation = 2**level
        picked = tokens // dilation
        start = offset_ref[level, head]
        order = table_ref[level - 1 : level, :]
        size = min(TILE, picked)
        for number in range(picked // size):
            rows = pl.ds(start + number * size * dilation, size, stride=dilation)
            query = q_f[rows, :].astype(BF16)
            scores = lax.dot_general(query, k_s[level - 1], NT, preferred_element_type=F32)
            at = lax.broadcasted_iota(jnp.int32, (size, tokens), 0) + number * size
            scores = jnp.where(order <= at, scores, LOW)
            m_old = m_s[rows, :]
            top = jnp.maximum(m_old[:, :1], jnp.max(scores, 1, keepdims=True))
            probs = jnp.exp2(scores - top).astype(BF16)
            both = jnp.dot(probs, v_s[level - 1], preferred_element_type=F32)
            factor = jnp.exp2(m_old - top)
            m_s[rows, :] = jnp.broadcast_to(top, (size, 128))
            a_s[rows, :] = factor * a_s[rows, :] + both[:, :128]
            l_s[rows, :] = factor * l_s[rows, :] + both[:, 128:]

    out_ref[...] = (a_s[...] / l_s[...]).astype(BF16)


def attend(q, state, exchanged, table, offsets, head_base):
    levels, heads = offsets.shape
    tokens = q.shape[0]
    half = heads // 2
    mine = pl.BlockSpec((tokens, 128), lambda h, offset: (0, h + head_base))

    def group_spec(array, shift):
        return pl.BlockSpec((array.shape[0], 128), lambda h, offset: (0, h + shift))

    return pl.pallas_call(
        functools.partial(attend_kernel, levels, head_base),
        grid_spec=pltpu.PrefetchScalarGridSpec(
            num_scalar_prefetch=1,
            grid=(half,),
            in_specs=[mine] * 4
            + [group_spec(a, head_base) for a in exchanged]
            + [group_spec(a, heads + head_base) for a in exchanged]
            + [whole_spec(table)],
            out_specs=pl.BlockSpec((tokens, 128), lambda h, offset: (0, h)),
            scratch_shapes=[
                pltpu.VMEM((tokens, 128), F32),
                pltpu.VMEM((levels - 1, tokens, 128), BF16),
                pltpu.VMEM((levels - 1, tokens, 256), BF16),
                pltpu.VMEM((tokens, 128), F32),
                pltpu.VMEM((tokens, 128), F32),
                pltpu.VMEM((tokens, 128), F32),
            ],
        ),
        out_shape=jax.ShapeDtypeStruct((tokens, 128 * half), BF16),
        compiler_params=pltpu.CompilerParams(vmem_limit_bytes=VMEM_LIMIT),
        cost_estimate=cost(CA),
        name="attend",
    )(offsets, q, *state, *exchanged, *exchanged, table)


def output_kernel(where, n_arrays, shares, *refs):
    owner_ref, refs = refs[0], refs[1:]
    arrays, refs = refs[:n_arrays], refs[n_arrays:]
    base_ref, w_ref, out_ref, x_s, w_s, piece_sems, w_sems = refs
    copies = copy_pieces(where, arrays, x_s, piece_sems)
    for number, share in enumerate(shares):
        source = w_ref.at[share : share + w_s.shape[1], owner_ref[number]]
        copies.append(pltpu.make_async_copy(source, w_s.at[number], w_sems.at[number]))
        copies[-1].start()
    for copy in copies:
        copy.wait()
    tile = 512
    rows, depth = x_s.shape

    @pl.loop(0, rows // tile)
    def _(n):
        at = pl.ds(pl.multiple_of(n * tile, tile), tile)
        weight = w_s[...].reshape(depth, out_ref.shape[1])
        total = jnp.dot(x_s[at, :], weight, preferred_element_type=F32)
        out_ref[at, :] = (base_ref[at, :].astype(F32) + total).astype(out_ref.dtype)


def output(parts, base, w_columns, dtype, us):
    pieces = [piece for part, _ in parts for piece in part]
    shares = [share for part, share in parts for _ in part]
    operands, where = split_pieces(pieces)
    rows, width = base.shape
    depth = w_columns.size // width // 16
    anywhere = pl.BlockSpec(memory_space=pl.ANY)
    vector = pl.BlockSpec(memory_space=pltpu.VMEM)
    return pl.pallas_call(
        functools.partial(output_kernel, where, len(operands), shares),
        in_specs=[pl.BlockSpec(memory_space=pltpu.SMEM)]
        + [anywhere] * len(operands)
        + [vector, anywhere],
        out_specs=vector,
        scratch_shapes=[
            pltpu.VMEM((rows, len(where) * depth), BF16),
            pltpu.VMEM((len(where), w_columns.shape[0] // 2) + w_columns.shape[2:], BF16),
            pltpu.SemaphoreType.DMA((len(where),)),
            pltpu.SemaphoreType.DMA((len(where),)),
        ],
        out_shape=jax.ShapeDtypeStruct((rows, width), dtype),
        compiler_params=pltpu.CompilerParams(vmem_limit_bytes=VMEM_LIMIT),
        cost_estimate=cost(us),
        name="output",
    )(piece_owners(pieces), *operands, base, w_columns)


def column_shares(w_out):
    seq = lax.axis_index("seq")
    share = seq // 4 * 2 + seq % 2
    rows = w_out.shape[0] // 8
    part = lax.dynamic_slice_in_dim(w_out, share * rows, rows, 0)
    width = w_out.shape[1] // 8
    cut = part.reshape(rows, 8, width).transpose(1, 0, 2)
    return lax.all_to_all(cut, "tp", 0, 0, tiled=True)


def gather_shares(mine):
    groups = [[y * 4 + x_lo * 2 + core for y in range(4) for core in range(2)] for x_lo in range(2)]
    return lax.all_gather(mine, "seq", axis=0, axis_index_groups=groups)


def after(value, *others):
    return lax.optimization_barrier((value, *others))[0]


def on_device(tokens, norm_gain, w_query, w_key, w_value, w_out, offsets):
    rows = tokens.shape[0]
    levels, heads = offsets.shape
    low = rows // 4
    weights = (w_key, w_value, w_query)

    t0, t1 = tokens[:low], tokens[low:]
    below0, above0 = z_shift(t0, 1), z_shift(t0, -1)
    other0, other1 = x_swap(t0), x_swap(t1)
    far0 = z_shift(below0, 1)
    pair1 = jnp.stack([t1, after(other1, below0, above0, far0)])
    below1, above1 = z_shift(pair1, 1), z_shift(pair1, -1)
    others0 = x_swap(jnp.stack([below0, above0, far0]))
    first = z_first_pieces(t0, below0, above0, far0, other0, others0)
    old = project(first, 0, rows, [], [], True, norm_gain, weights, offsets, C0)
    if F1:
        below1 = after(below1, old[1])
    far1 = z_shift(below1[0], 1), z_shift(above1[1], -1)
    mine = column_shares(after(w_out, far0))
    second = x_first_pieces(pair1, after(below1, mine), above1, *far1)
    sums = project(second[:6], low, rows, [], [], False, norm_gain, weights, offsets, C1)
    old = project(second[6:], low, rows, sums, old, True, norm_gain, weights, offsets, C2)
    k, v, q = old[:3]
    exchanged = first_exchange(*old[3:])
    state = attend_local(q, k, v)
    exchanged = second_exchange(*exchanged, state[0])
    table = key_table(rows // 16, levels)
    gathered = []
    att_a = attend(q, state, exchanged, table, offsets, 0)
    w_columns = gather_shares(after(mine, att_a))
    below_a, above_a, other_a = z_shift(att_a, 1), z_shift(att_a, -1), x_swap(att_a)
    if F5:
        q = after(q, att_a)
    att_b = attend(q, state, exchanged, table, offsets, heads // 2)
    far_a = z_shift(below_a, 1)
    other_b = x_swap(att_b)
    if F3:
        other_b = after(other_b, below_a, above_a)
    if F4:
        below_a = after(below_a, other_a)
    pair_b = jnp.stack([att_b, other_b])
    if F8:
        others_a = x_swap(jnp.stack([below_a, above_a]))
        if F9:
            far_a = after(far_a, others_a)
        other_far_a = x_swap(far_a)
    else:
        others_a, other_far_a = x_swap(jnp.stack([below_a, above_a, far_a])), None
    below_b, above_b = z_shift(pair_b, 1), z_shift(pair_b, -1)
    far_b = z_shift(below_b[0], 1), z_shift(above_b[1], -1)
    gathered = [
        z_first_pieces(att_a, below_a, above_a, far_a, other_a, others_a, other_far_a),
        x_first_pieces(pair_b, below_b, above_b, *far_b),
    ]
    heads_a, heads_b = gathered
    total = output([(heads_a[:4], 0)], tokens, w_columns, F32, CX)
    total = output([(heads_b[:6], 4)], total, w_columns, F32, CX)
    return output([(heads_b[6:], 4), (heads_a[4:], 0)], total, w_columns, BF16, CO)


def solution(mesh):
    placed = (
        P("seq", "tp"),
        P(),
        P(None, "tp"),
        P(None, "tp"),
        P(None, "tp"),
        P("tp", None),
        P(None, "tp"),
    )
    return jax.shard_map(
        on_device, mesh=mesh, in_specs=placed, out_specs=P("seq", "tp"), check_vma=False
    )
```
